32 devices in a mesh: slab: 8 (over y, x, core), probe: 4 (over z).
Axes of the slice: x: 2, y: 2, z: 4, core: 2. Of those that a mesh axis runs over, the one named last changes fastest.
Arguments:
- probes: float32 [8, 3, 16, 128, 128], P('probe', None, 'slab'), may hold values from -50 to 50
- earlier: float32 [16, 3, 16, 128, 128], P(None, None, 'slab', 'probe'), may hold values from -16 to 16
- modulus: float32 [16, 128, 128], P('slab'), may hold values from 0.5 to 2
- tangent: float32 [6, 16, 128, 128], P(None, 'slab'), may hold values from -0.3 to 2, as said below
Outputs:
- basis: float32 [8, 3, 16, 128, 128], P('probe', None, 'slab')
- correlation: float32 [16, 8], replicated
The draws below stay inside these ranges and needn't reach their ends.
Inputs may be any that keep to these rules, and one draw needn't show every extreme that they name: `tangent`: entries 0 to 2 lie in 1 to 2, entries 3 to 5 in -0.3 to 0.3.
All inputs are finite; a program needn't handle non-finite values.
Results may differ from the reference program's by a relative error of at most 0.00014.
Values sent between devices are 32-bit elements; how exact they have to be, the bound alone decides.
A program may use at most 64 MiB of HBM per device.

```python
import math
import jax
import jax.numpy as jnp
from jax import lax

NY = 128
NX = 128
EARLIER = 16
NZ = 16
PROBES = 8


def draw_probes(key, part):
    subkeys = jax.random.split(key, 3)
    extent = (PROBES, 3, NZ, NY, NX)
    column_scale = 10.0 ** jax.random.uniform(subkeys[1], (PROBES, 1, 1, 1, 1), jnp.float32, -0.5, 0.5)
    row_scale = 10.0 ** jax.random.uniform(subkeys[2], (1, 1, NZ, NY, 1), jnp.float32, -0.5, 0.5)
    values = jnp.clip(jax.random.normal(subkeys[0], extent, jnp.float32), -5.0, 5.0)
    return values * column_scale * row_scale


def draw_earlier(key, part):
    subkeys = jax.random.split(key, 2)
    extent = (EARLIER, 3, NZ, NY, NX)
    column_scale = 10.0 ** jax.random.uniform(subkeys[1], (EARLIER, 1, 1, 1, 1), jnp.float32, -0.5, 0.5)
    values = jnp.clip(jax.random.normal(subkeys[0], extent, jnp.float32), -5.0, 5.0)
    return values * column_scale


def draw_tangent(key, part):
    uniform_part = jax.random.uniform(key, (6, NZ, NY, NX), jnp.float32, 0.0, 1.0)
    diagonal_part = 1.0 + uniform_part[0:3]
    coupling = 0.6 * uniform_part[3:6] - 0.3
    return jnp.concatenate([diagonal_part, coupling], axis=0)


def levels(rng, shape, shards, least, largest):
    def one(dim, parts):
        draws = jax.random.uniform(jax.random.fold_in(jax.random.fold_in(rng, 6), dim), (parts,), jnp.float32, least / len(shards), largest / len(shards))
        return jnp.repeat(jnp.exp(draws), shape[dim] // parts).reshape((-1,) + (1,) * (len(shape) - dim - 1))

    gain = one(*shards[0])
    for cut in shards[1:]:
        gain = gain * one(*cut)
    return gain


def setup_inputs(seed: int = 0) -> dict:
    arg_keys = jax.random.split(jax.random.key(seed), 5)
    return {
        "probes": draw_probes(jax.random.fold_in(arg_keys[4], 71), 0),
        "earlier": draw_earlier(jax.random.fold_in(arg_keys[4], 71), 0),
        "modulus": jnp.clip(jnp.exp(math.log(2.0) - 1.3862944 * jax.random.uniform(arg_keys[2], (NZ, NY, NX), jnp.float32) ** levels(arg_keys[2], (NZ, NY, NX), ((0, 8),), -0.2, 0.2)), 0.5, 2.0),
        "tangent": draw_tangent(jax.random.fold_in(arg_keys[4], 71), 0),
    }


def scaled_tangent(vectors, modulus, tensor):
    planes = vectors.shape[2] - 2
    height = vectors.shape[3]
    breadth = vectors.shape[4]
    padded = jnp.pad(vectors, ((0, 0), (0, 0), (0, 0), (1, 1), (1, 1)))
    mod_pad = jnp.pad(modulus, ((0, 0), (1, 1), (1, 1)))
    centre = padded[:, :, 1:planes + 1, 1:height + 1, 1:breadth + 1]
    mod_centre = mod_pad[1:planes + 1, 1:height + 1, 1:breadth + 1]
    summed = jnp.zeros_like(centre)
    for step_z in (-1, 0, 1):
        for step_y in (-1, 0, 1):
            for step_x in (-1, 0, 1):
                reach = abs(step_z) + abs(step_y) + abs(step_x)
                if reach == 0:
                    continue
                weight = (0.3, 0.1, 0.05)[reach - 1]
                nearby = padded[:, :, 1 + step_z:planes + 1 + step_z, 1 + step_y:height + 1 + step_y, 1 + step_x:breadth + 1 + step_x]
                mod_near = mod_pad[1 + step_z:planes + 1 + step_z, 1 + step_y:height + 1 + step_y, 1 + step_x:breadth + 1 + step_x]
                edge_coef = 0.5 * weight * (mod_centre + mod_near)
                summed = summed + edge_coef * (centre - nearby)
    first_c = centre[:, 0]
    second_c = centre[:, 1]
    third_c = centre[:, 2]
    local_part = jnp.stack([tensor[0] * first_c + tensor[3] * second_c + tensor[4] * third_c, tensor[3] * first_c + tensor[1] * second_c + tensor[5] * third_c, tensor[4] * first_c + tensor[5] * second_c + tensor[2] * third_c], axis=1)
    return (summed + local_part - 8.0 * centre) / 8.0

def pad_planes(values):
    return jnp.pad(values, ((0, 0), (0, 0), (1, 1), (0, 0), (0, 0)))

def reference(probes, earlier, modulus, tangent):
    mod_padded = jnp.pad(modulus, ((1, 1), (0, 0), (0, 0)))

    def filter_one(single):
        single = single[None]
        first = scaled_tangent(pad_planes(single), mod_padded, tangent)
        second = scaled_tangent(pad_planes(first), mod_padded, tangent)
        return (2.0 * second - single)[0]
    filtered = lax.map(filter_one, probes)
    highest = lax.Precision.HIGHEST
    flat_y = filtered.reshape(filtered.shape[0], -1)
    flat_q = earlier.reshape(earlier.shape[0], -1)
    gram_earlier = jnp.dot(flat_q, flat_q.T, precision=highest)
    cross = jnp.dot(flat_q, flat_y.T, precision=highest)
    factor = jnp.linalg.cholesky(gram_earlier)
    coeff = jax.scipy.linalg.cho_solve((factor, True), cross)
    residue = flat_y - jnp.dot(coeff.T, flat_q, precision=highest)
    gram = jnp.dot(residue, residue.T, precision=highest)
    lower = jnp.linalg.cholesky(gram)
    scale = jnp.sqrt(jnp.float32(3 * NZ * NY * NX))
    basis = jax.scipy.linalg.solve_triangular(lower, residue, lower=True) * scale
    return (basis.reshape(filtered.shape), coeff * scale)
```

```python
import functools

import jax
import jax.numpy as jnp
from jax import lax
from jax.experimental import pallas as pl
from jax.experimental.pallas import tpu as pltpu
from jax.sharding import PartitionSpec as P

MESH = pl.DeviceIdType.MESH
LANES = 128
PAD = 8
GROUP = 4


def neighbour_sum(ref, lead, z, start, rows):
    def at(plane, off):
        return ref[lead + (plane, pl.ds(PAD + start + off, rows), slice(None))]

    centre = at(z, 0)
    beside = at(z, -1) + at(z, 1)
    above = at(z - 1, 0) + at(z + 1, 0)
    corner = (at(z - 1, -1) + at(z + 1, -1)) + (at(z - 1, 1) + at(z + 1, 1))
    along = 0.3 * centre + 0.1 * (above + beside) + 0.05 * corner
    still = 0.3 * (above + beside) + 0.1 * corner
    width = along.shape[-1]
    lane = lax.broadcasted_iota(jnp.int32, along.shape, 1)
    from_left = jnp.where(lane == 0, 0.0, pltpu.roll(along, 1, 1))
    from_right = jnp.where(lane == width - 1, 0.0, pltpu.roll(along, width - 1, 1))
    return still + from_left + from_right


def spread(column, shape):
    return jnp.broadcast_to(column, shape)


def kernel(
    slabs, groups, scale,
    probes_ref, earlier_ref, modulus_ref, tangent_ref,
    basis_ref, corr_ref,
    v0, v1, g0, g1, mod, ten, diag, quick, filt, every, outgoing,
    acc_q, acc_y, slots_q, slots_qp, slots_y, slots_yp, inverse, mixing,
    load_sem, halo_send, halo_recv, mod_send, mod_recv,
    there_send, there_recv, back_send, back_recv,
    sum_send, sum_recv, sump_send, sump_recv, own_sem,
):
    slab = lax.axis_index("slab")
    group = lax.axis_index("probe")
    mine, _, depth, height, _ = probes_ref.shape
    known, fields, share, _ = earlier_ref.shape
    total = mine * groups
    rows = 32

    loads = [
        pltpu.make_async_copy(modulus_ref, mod.at[pl.ds(1, depth), pl.ds(PAD, height), :], load_sem.at[0]),
        pltpu.make_async_copy(tangent_ref, ten, load_sem.at[1]),
        pltpu.make_async_copy(earlier_ref, quick, load_sem.at[2]),
    ]
    for r in range(mine):
        loads.append(
            pltpu.make_async_copy(
                probes_ref.at[r],
                v0.at[r, :, pl.ds(1, depth), pl.ds(PAD, height), :],
                load_sem.at[3 + r],
            )
        )
    for copy in loads:
        copy.start()

    barrier = pltpu.get_barrier_semaphore()
    for o in range(1, slabs):
        pl.semaphore_signal(barrier, inc=1, device_id={"slab": lax.rem(slab + o, slabs)}, device_id_type=MESH)
    for o in range(1, groups):
        pl.semaphore_signal(barrier, inc=1, device_id={"probe": lax.rem(group + o, groups)}, device_id_type=MESH)

    for ref in (v0, v1):
        edge = jnp.zeros(ref.shape[:3] + (PAD, LANES), jnp.float32)
        ref[:, :, :, pl.ds(0, PAD), :] = edge
        ref[:, :, :, pl.ds(PAD + height, PAD), :] = edge
    edge = jnp.zeros((depth + 2, PAD, LANES), jnp.float32)
    mod[:, pl.ds(0, PAD), :] = edge
    mod[:, pl.ds(PAD + height, PAD), :] = edge

    def clear(plane):
        for ref in (v0, v1):
            ref[:, :, plane, pl.ds(PAD, height), :] = jnp.zeros((mine, 3, height, LANES), jnp.float32)
        mod[plane, pl.ds(PAD, height), :] = jnp.zeros((height, LANES), jnp.float32)

    @pl.when(slab == 0)
    def _():
        clear(0)

    @pl.when(slab == slabs - 1)
    def _():
        clear(depth + 1)

    pl.semaphore_wait(barrier, slabs + groups - 2)

    towards = (lax.rem(slab + slabs - 1, slabs), lax.rem(slab + 1, slabs))
    can_send = (slab > 0, slab < slabs - 1)
    can_recv = (slab < slabs - 1, slab > 0)
    lands = (depth + 1, 0)

    def mod_copy(way):
        return pltpu.make_async_remote_copy(
            src_ref=modulus_ref.at[(0, depth - 1)[way]],
            dst_ref=mod.at[lands[way], pl.ds(PAD, height), :],
            send_sem=mod_send.at[way],
            recv_sem=mod_recv.at[way],
            device_id={"slab": towards[way]},
            device_id_type=MESH,
        )

    def halo_copy(stage, r, way):
        if stage == 0:
            source, into = probes_ref.at[r, :, (0, depth - 1)[way]], v0
        else:
            source, into = v1.at[r, :, (1, depth)[way], pl.ds(PAD, height), :], v1
        return pltpu.make_async_remote_copy(
            src_ref=source,
            dst_ref=into.at[r, :, lands[way], pl.ds(PAD, height), :],
            send_sem=halo_send.at[stage, r, way],
            recv_sem=halo_recv.at[stage, r, way],
            device_id={"slab": towards[way]},
            device_id_type=MESH,
        )

    def guarded(condition, act):
        @pl.when(condition)
        def _():
            act()

    for way in range(2):
        def begin(way=way):
            mod_copy(way).start()
            for r in range(mine):
                halo_copy(0, r, way).start()
        guarded(can_send[way], begin)

    def products(first, second, acc_ref, rows_at, cols_at, mirror_at):
        def step(f, accs):
            left = [ref[k, f] for ref, k in first]
            right = [ref[k, f] for ref, k in second]
            out = []
            n = 0
            for a in left:
                for b in right:
                    prod = a * b
                    part = accs[n]
                    for t in range(share // 8):
                        part = part + prod[8 * t : 8 * t + 8]
                    out.append(part)
                    n += 1
            return tuple(out)

        zero = jnp.zeros((8, LANES), jnp.float32)
        accs = lax.fori_loop(0, fields, step, (zero,) * (len(first) * len(second)))
        n = 0
        for i in range(len(first)):
            for j in range(len(second)):
                acc_ref[cols_at[i], rows_at[j]] = accs[n]
                if mirror_at is not None:
                    col, row = mirror_at(i, j)
                    acc_ref[col, row] = accs[n]
                n += 1

    def collapse(acc_ref, cols, count):
        lane = lax.broadcasted_iota(jnp.int32, (count, LANES), 1)
        result = jnp.zeros((count, LANES), jnp.float32)
        for v in range(cols):
            summed = jnp.sum(jnp.sum(acc_ref[v], axis=1), axis=1, keepdims=True)
            result = jnp.where(lane == v, spread(summed, (count, LANES)), result)
        return result

    def share_copy(slots, axis, me, count, o, sends, recvs):
        return pltpu.make_async_remote_copy(
            src_ref=slots.at[me],
            dst_ref=slots.at[me],
            send_sem=sends.at[o],
            recv_sem=recvs.at[o],
            device_id={axis: lax.rem(me + o, count)},
            device_id_type=MESH,
        )

    def share_start(slots, axis, me, count, sends, recvs, value):
        slots[me] = value
        for o in range(1, count):
            share_copy(slots, axis, me, count, o, sends, recvs).start()

    def share_finish(slots, axis, me, count, sends, recvs):
        for o in range(1, count):
            share_copy(slots, axis, me, count, o, sends, recvs).wait()
        value = slots[0]
        for i in range(1, count):
            value = value + slots[i]
        return value

    loads[2].wait()
    for i in range(0, known, GROUP):
        for j in range(i, known, GROUP):
            left = list(range(i, i + GROUP))
            right = list(range(j, j + GROUP))
            products(
                [(quick, k) for k in left], [(quick, k) for k in right], acc_q, right, left,
                (lambda a, b, left=left, right=right: (right[b], left[a])) if i != j else None,
            )
    share_start(slots_q, "slab", slab, slabs, sum_send.at[0], sum_recv.at[0], collapse(acc_q, known, known))

    loads[0].wait()
    loads[1].wait()
    for way in range(2):
        guarded(can_recv[way], lambda way=way: mod_copy(way).wait_recv())

    def coefficients(z, carry):
        for start in range(0, height, rows):
            here = pl.ds(start, rows)
            m = mod[z + 1, pl.ds(PAD + start, rows), :]
            base = (3.4 * m + neighbour_sum(mod, (), z + 1, start, rows)) * 0.0625 - 1.0
            for c in range(3):
                diag[c, z, here, :] = base + 0.125 * ten[c, z, here, :]
        return carry

    lax.fori_loop(0, depth, coefficients, 0)

    def halo_products(stage, r, way):
        v, g = ((v0, g0), (v1, g1))[stage]
        plane = lands[way]
        for c in range(3):
            g[r, c, plane] = mod[plane] * v[r, c, plane]

    def apply(stage, r):
        v, g = ((v0, g0), (v1, g1))[stage]

        def body(z, carry):
            for start in range(0, height, rows):
                here = pl.ds(start, rows)
                inner = pl.ds(PAD + start, rows)
                m = mod[z + 1, inner, :]
                vec = [v[r, c, z + 1, inner, :] for c in range(3)]
                cross = [0.125 * ten[3 + c, z, here, :] for c in range(3)]
                mixed = (
                    cross[0] * vec[1] + cross[1] * vec[2],
                    cross[0] * vec[0] + cross[2] * vec[2],
                    cross[1] * vec[0] + cross[2] * vec[1],
                )
                for c in range(3):
                    out = diag[c, z, here, :] * vec[c] + mixed[c]
                    near = m * neighbour_sum(v, (r, c), z + 1, start, rows) + neighbour_sum(
                        g, (r, c), z + 1, start, rows
                    )
                    out = out - 0.0625 * near
                    if stage == 0:
                        v1[r, c, z + 1, inner, :] = out
                        g1[r, c, z + 1, inner, :] = m * out
                    else:
                        filt[r, c * depth + z, here, :] = 2.0 * out - v0[r, c, z + 1, inner, :]
            return carry

        lax.fori_loop(0, depth, body, 0)

    def wait_halo(stage, r):
        for way in range(2):
            guarded(can_recv[way], lambda way=way: halo_copy(stage, r, way).wait_recv())
            halo_products(stage, r, way)

    for r in range(mine):
        loads[3 + r].wait()
        for c in range(3):
            for z in range(1, depth + 1):
                g0[r, c, z] = mod[z] * v0[r, c, z]
                blank = jnp.zeros((PAD, LANES), jnp.float32)
                g1[r, c, z, pl.ds(0, PAD), :] = blank
                g1[r, c, z, pl.ds(PAD + height, PAD), :] = blank
        wait_halo(0, r)
        apply(0, r)
        for way in range(2):
            guarded(can_send[way], lambda way=way, r=r: halo_copy(1, r, way).start())

    partial = share_finish(slots_q, "slab", slab, slabs, sum_send.at[0], sum_recv.at[0])
    share_start(slots_qp, "probe", group, groups, sump_send.at[0], sump_recv.at[0], partial)

    order = sorted(range(1, groups), key=lambda o: (abs(o - groups // 2), o))

    def there_copy(r, o):
        to = lax.rem(group + o, groups)
        return pltpu.make_async_remote_copy(
            src_ref=filt.at[r, :, pl.ds(pl.multiple_of(to * share, share), share), :],
            dst_ref=every.at[group * mine + r],
            send_sem=there_send.at[r, o],
            recv_sem=there_recv.at[r, o],
            device_id={"probe": to},
            device_id_type=MESH,
        )

    own_rows = pl.ds(pl.multiple_of(group * share, share), share)
    for r in range(mine):
        wait_halo(1, r)
        apply(1, r)
        for o in order:
            there_copy(r, o).start()
        keep = pltpu.make_async_copy(filt.at[r, :, own_rows, :], every.at[group * mine + r], own_sem.at[r])
        keep.start()

    gram_q = share_finish(slots_qp, "probe", group, groups, sump_send.at[0], sump_recv.at[0])
    square = (known, LANES)
    lane = lax.broadcasted_iota(jnp.int32, square, 1)
    line = lax.broadcasted_iota(jnp.int32, square, 0)
    table = jnp.where(lane < known, gram_q, 0.0) + jnp.where(lane == line + known, 1.0, 0.0)
    for k in range(known):
        column = spread(table[:, k : k + 1], square)
        pivot = spread(column[k : k + 1, :], square)
        lead = spread(table[k : k + 1, :], square) / pivot
        table = jnp.where(line == k, lead, table - column * lead)
    inverse[...] = pltpu.roll(table, LANES - known, 1)
    inv = jnp.where(lane < known, inverse[...], 0.0)
    inverse[...] = inv

    def batch(r):
        ids = [p * mine + r for p in range(groups)]
        return [ids[i : i + GROUP] for i in range(0, groups, GROUP)]

    for r in range(mine):
        pltpu.make_async_copy(filt.at[r, :, own_rows, :], every.at[group * mine + r], own_sem.at[r]).wait()
        for o in order:
            there_copy(r, o).wait_recv()
        for ids in batch(r):
            for i in range(0, known, GROUP):
                left = list(range(i, i + GROUP))
                products([(quick, k) for k in left], [(every, k) for k in ids], acc_y, ids, left, None)
            for before in range(r + 1):
                for old in batch(before):
                    if before == r and old[0] > ids[0]:
                        continue
                    same = old == ids
                    products(
                        [(every, k) for k in old], [(every, k) for k in ids], acc_y, ids,
                        [known + k for k in old],
                        None if same else (lambda a, b, old=old, ids=ids: (known + ids[b], old[a])),
                    )
    part = collapse(acc_y, known + total, total)
    share_start(slots_y, "slab", slab, slabs, sum_send.at[1], sum_recv.at[1], part)
    part = share_finish(slots_y, "slab", slab, slabs, sum_send.at[1], sum_recv.at[1])
    share_start(slots_yp, "probe", group, groups, sump_send.at[1], sump_recv.at[1], part)
    gram_y = share_finish(slots_yp, "probe", group, groups, sump_send.at[1], sump_recv.at[1])

    flat = (total, LANES)
    lane = lax.broadcasted_iota(jnp.int32, flat, 1)
    line = lax.broadcasted_iota(jnp.int32, flat, 0)
    cross = jnp.where(lane < known, gram_y, 0.0)
    coeff = jnp.zeros(flat, jnp.float32)
    for k in range(known):
        coeff = coeff + spread(cross[:, k : k + 1], flat) * spread(inverse[k : k + 1, :], flat)
    nt = (((1,), (1,)), ((), ()))
    taken = lax.dot_general(
        coeff, jnp.concatenate([cross, jnp.zeros((LANES - total, LANES), jnp.float32)], axis=0), nt,
        precision=lax.Precision.HIGHEST, preferred_element_type=jnp.float32,
    )
    at = known + total
    gram = pltpu.roll(gram_y, LANES - known, 1) - taken
    gram = jnp.where(lane < total, gram, 0.0)
    work = pltpu.roll(gram, at, 1) + jnp.where(lane == line + known, 1.0, 0.0) - coeff
    factor = jnp.ones(flat, jnp.float32)
    for k in range(total):
        column = spread(work[:, at + k : at + k + 1], flat)
        pivot = spread(column[k : k + 1, :], flat)
        lead = spread(work[k : k + 1, :], flat) / pivot
        factor = jnp.where(line == k, pivot, factor)
        work = jnp.where(line > k, work - column * lead, work)
    mixing[...] = work * (scale / jnp.sqrt(factor))

    def make(i):
        weights = mixing[pl.ds(i, 1), :]
        splats = [spread(weights[:, v : v + 1], (8, LANES)) for v in range(known + total)]

        def step(f, carry):
            for t in range(share // 8):
                sub = pl.ds(8 * t, 8)
                value = splats[0] * quick[0, f, sub, :]
                for v in range(1, known):
                    value = value + splats[v] * quick[v, f, sub, :]
                for v in range(total):
                    value = value + splats[known + v] * every[v, f, sub, :]
                outgoing[i, f, sub, :] = value
            return carry

        lax.fori_loop(0, fields, step, 0)

    def back_copy(r, o):
        to = lax.rem(group + o, groups)
        return pltpu.make_async_remote_copy(
            src_ref=outgoing.at[to * mine + r],
            dst_ref=basis_ref.at[r, :, own_rows, :],
            send_sem=back_send.at[r, o],
            recv_sem=back_recv.at[r, o],
            device_id={"probe": to},
            device_id_type=MESH,
        )

    def own_copy(r):
        return pltpu.make_async_copy(
            outgoing.at[group * mine + r], basis_ref.at[r, :, own_rows, :], own_sem.at[mine + r]
        )

    for o in order:
        for r in range(mine):
            make(lax.rem(group + o, groups) * mine + r)
            back_copy(r, o).start()
    for r in range(mine):
        make(group * mine + r)
        own_copy(r).start()

    corr = lax.dot_general(
        inverse[...], cross, nt, precision=lax.Precision.HIGHEST, preferred_element_type=jnp.float32
    )
    corr_ref[...] = corr * scale

    for way in range(2):
        def finish(way=way):
            mod_copy(way).wait_send()
            for stage in range(2):
                for r in range(mine):
                    halo_copy(stage, r, way).wait_send()
        guarded(can_send[way], finish)
    for r in range(mine):
        own_copy(r).wait()
        for o in order:
            there_copy(r, o).wait_send()
            back_copy(r, o).wait()


def body(probes, earlier, modulus, tangent):
    mine, parts, depth, height, width = probes.shape
    known, _, _, share, _ = earlier.shape
    slabs = lax.axis_size("slab")
    groups = lax.axis_size("probe")
    total = mine * groups
    fields = parts * depth
    scale = float(parts * depth * slabs * height * width) ** 0.5
    f32 = jnp.float32
    padded = (mine, parts, depth + 2, height + 2 * PAD, width)
    dma = pltpu.SemaphoreType.DMA
    anywhere = pl.BlockSpec(memory_space=pl.ANY)
    basis, corr = pl.pallas_call(
        functools.partial(kernel, slabs, groups, scale),
        out_shape=(
            jax.ShapeDtypeStruct((mine, fields, height, width), f32),
            jax.ShapeDtypeStruct((known, total), f32),
        ),
        in_specs=[anywhere] * 4,
        out_specs=(anywhere, pl.BlockSpec(memory_space=pltpu.VMEM)),
        scratch_shapes=[
            pltpu.VMEM(padded, f32),
            pltpu.VMEM(padded, f32),
            pltpu.VMEM(padded, f32),
            pltpu.VMEM(padded, f32),
            pltpu.VMEM((depth + 2, height + 2 * PAD, width), f32),
            pltpu.VMEM((6, depth, height, width), f32),
            pltpu.VMEM((3, depth, height, width), f32),
            pltpu.VMEM((known, fields, share, width), f32),
            pltpu.VMEM((mine, fields, height, width), f32),
            pltpu.VMEM((total, fields, share, width), f32),
            pltpu.VMEM((total, fields, share, width), f32),
            pltpu.VMEM((known, known, 8, width), f32),
            pltpu.VMEM((known + total, total, 8, width), f32),
            pltpu.VMEM((slabs, known, LANES), f32),
            pltpu.VMEM((groups, known, LANES), f32),
            pltpu.VMEM((slabs, total, LANES), f32),
            pltpu.VMEM((groups, total, LANES), f32),
            pltpu.VMEM((known, LANES), f32),
            pltpu.VMEM((total, LANES), f32),
            dma((3 + mine,)),
            dma((2, mine, 2)),
            dma((2, mine, 2)),
            dma((2,)),
            dma((2,)),
            dma((mine, groups)),
            dma((mine, groups)),
            dma((mine, groups)),
            dma((mine, groups)),
            dma((2, slabs)),
            dma((2, slabs)),
            dma((2, groups)),
            dma((2, groups)),
            dma((2 * mine,)),
        ],
        compiler_params=pltpu.CompilerParams(
            collective_id=0, has_side_effects=True, vmem_limit_bytes=40 * 1024 * 1024
        ),
    )(probes, earlier.reshape(known, fields, share, width), modulus, tangent)
    return basis.reshape(probes.shape), corr


def solution(mesh):
    in_specs = (
        P("probe", None, "slab", None, None),
        P(None, None, "slab", "probe", None),
        P("slab", None, None),
        P(None, "slab", None, None),
    )
    out_specs = (P("probe", None, "slab", None, None), P())
    return jax.shard_map(body, mesh=mesh, in_specs=in_specs, out_specs=out_specs, check_vma=False)
```

```python
import functools

import jax
import jax.numpy as jnp
from jax import lax
from jax.experimental import pallas as pl
from jax.experimental.pallas import tpu as pltpu
from jax.sharding import PartitionSpec as P

MESH = pl.DeviceIdType.MESH
LANES = 128
PAD = 8
GROUP = 4


def neighbour_sum(ref, lead, z, start, rows):
    def at(plane, off):
        return ref[lead + (plane, pl.ds(PAD + start + off, rows), slice(None))]

    centre = at(z, 0)
    beside = at(z, -1) + at(z, 1)
    above = at(z - 1, 0) + at(z + 1, 0)
    corner = (at(z - 1, -1) + at(z + 1, -1)) + (at(z - 1, 1) + at(z + 1, 1))
    along = 0.3 * centre + 0.1 * (above + beside) + 0.05 * corner
    still = 0.3 * (above + beside) + 0.1 * corner
    width = along.shape[-1]
    lane = lax.broadcasted_iota(jnp.int32, along.shape, 1)
    from_left = jnp.where(lane == 0, 0.0, pltpu.roll(along, 1, 1))
    from_right = jnp.where(lane == width - 1, 0.0, pltpu.roll(along, width - 1, 1))
    return still + from_left + from_right


def spread(column, shape):
    return jnp.broadcast_to(column, shape)


def kernel(
    slabs, groups, scale,
    probes_ref, earlier_ref, modulus_ref, tangent_ref,
    basis_ref, corr_ref,
    v0, v1, g0, g1, mod, ten, diag, quick, filt, every, outgoing,
    acc_q, acc_y, slots_q, slots_qp, slots_y, slots_yp, inverse, mixing,
    load_sem, halo_send, halo_recv, mod_send, mod_recv,
    there_send, there_recv, back_send, back_recv,
    sum_send, sum_recv, sump_send, sump_recv, own_sem,
):
    slab = lax.axis_index("slab")
    group = lax.axis_index("probe")
    mine, _, depth, height, _ = probes_ref.shape
    known, fields, share, _ = earlier_ref.shape
    total = mine * groups
    rows = 32

    loads = [
        pltpu.make_async_copy(modulus_ref, mod.at[pl.ds(1, depth), pl.ds(PAD, height), :], load_sem.at[0]),
        pltpu.make_async_copy(tangent_ref, ten, load_sem.at[1]),
        pltpu.make_async_copy(earlier_ref, quick, load_sem.at[2]),
    ]
    for r in range(mine):
        loads.append(
            pltpu.make_async_copy(
                probes_ref.at[r],
                v0.at[r, :, pl.ds(1, depth), pl.ds(PAD, height), :],
                load_sem.at[3 + r],
            )
        )
    for copy in loads:
        copy.start()

    barrier = pltpu.get_barrier_semaphore()
    for o in range(1, slabs):
        pl.semaphore_signal(barrier, inc=1, device_id={"slab": lax.rem(slab + o, slabs)}, device_id_type=MESH)
    for o in range(1, groups):
        pl.semaphore_signal(barrier, inc=1, device_id={"probe": lax.rem(group + o, groups)}, device_id_type=MESH)

    for ref in (v0, v1):
        edge = jnp.zeros(ref.shape[:3] + (PAD, LANES), jnp.float32)
        ref[:, :, :, pl.ds(0, PAD), :] = edge
        ref[:, :, :, pl.ds(PAD + height, PAD), :] = edge
    edge = jnp.zeros((depth + 2, PAD, LANES), jnp.float32)
    mod[:, pl.ds(0, PAD), :] = edge
    mod[:, pl.ds(PAD + height, PAD), :] = edge

    def clear(plane):
        for ref in (v0, v1):
            ref[:, :, plane, pl.ds(PAD, height), :] = jnp.zeros((mine, 3, height, LANES), jnp.float32)
        mod[plane, pl.ds(PAD, height), :] = jnp.zeros((height, LANES), jnp.float32)

    @pl.when(slab == 0)
    def _():
        clear(0)

    @pl.when(slab == slabs - 1)
    def _():
        clear(depth + 1)

    pl.semaphore_wait(barrier, slabs + groups - 2)

    towards = (lax.rem(slab + slabs - 1, slabs), lax.rem(slab + 1, slabs))
    can_send = (slab > 0, slab < slabs - 1)
    can_recv = (slab < slabs - 1, slab > 0)
    lands = (depth + 1, 0)

    def mod_copy(way):
        return pltpu.make_async_remote_copy(
            src_ref=modulus_ref.at[(0, depth - 1)[way]],
            dst_ref=mod.at[lands[way], pl.ds(PAD, height), :],
            send_sem=mod_send.at[way],
            recv_sem=mod_recv.at[way],
            device_id={"slab": towards[way]},
            device_id_type=MESH,
        )

    def halo_copy(stage, r, c, way):
        if stage == 0:
            source, into = probes_ref.at[r, c, (0, depth - 1)[way]], v0
        else:
            source, into = v1.at[r, c, (1, depth)[way], pl.ds(PAD, height), :], v1
        return pltpu.make_async_remote_copy(
            src_ref=source,
            dst_ref=into.at[r, c, lands[way], pl.ds(PAD, height), :],
            send_sem=halo_send.at[stage, r, c, way],
            recv_sem=halo_recv.at[stage, r, c, way],
            device_id={"slab": towards[way]},
            device_id_type=MESH,
        )

    def guarded(condition, act):
        @pl.when(condition)
        def _():
            act()

    def send_probe(r):
        for way in range(2):
            def begin(way=way):
                if r == 0:
                    mod_copy(way).start()
                for c in range(3):
                    halo_copy(0, r, c, way).start()
            guarded(can_send[way], begin)

    send_probe(0)

    def products(first, second, acc_ref, rows_at, cols_at, mirror_at):
        def step(f, accs):
            left = [ref[k, f] for ref, k in first]
            right = [ref[k, f] for ref, k in second]
            out = []
            n = 0
            for a in left:
                for b in right:
                    prod = a * b
                    part = accs[n]
                    for t in range(share // 8):
                        part = part + prod[8 * t : 8 * t + 8]
                    out.append(part)
                    n += 1
            return tuple(out)

        zero = jnp.zeros((8, LANES), jnp.float32)
        accs = lax.fori_loop(0, fields, step, (zero,) * (len(first) * len(second)))
        n = 0
        for i in range(len(first)):
            for j in range(len(second)):
                acc_ref[cols_at[i], rows_at[j]] = accs[n]
                if mirror_at is not None:
                    col, row = mirror_at(i, j)
                    acc_ref[col, row] = accs[n]
                n += 1

    def collapse(acc_ref, cols, count):
        lane = lax.broadcasted_iota(jnp.int32, (count, LANES), 1)
        result = jnp.zeros((count, LANES), jnp.float32)
        for v in range(cols):
            summed = jnp.sum(jnp.sum(acc_ref[v], axis=1), axis=1, keepdims=True)
            result = jnp.where(lane == v, spread(summed, (count, LANES)), result)
        return result

    def share_copy(slots, axis, me, count, o, sends, recvs):
        return pltpu.make_async_remote_copy(
            src_ref=slots.at[me],
            dst_ref=slots.at[me],
            send_sem=sends.at[o],
            recv_sem=recvs.at[o],
            device_id={axis: lax.rem(me + o, count)},
            device_id_type=MESH,
        )

    def share_start(slots, axis, me, count, sends, recvs, value):
        slots[me] = value
        for o in range(1, count):
            share_copy(slots, axis, me, count, o, sends, recvs).start()

    def share_finish(slots, axis, me, count, sends, recvs):
        for o in range(1, count):
            share_copy(slots, axis, me, count, o, sends, recvs).wait()
        value = slots[0]
        for i in range(1, count):
            value = value + slots[i]
        return value

    loads[2].wait()
    for i in range(0, known, GROUP):
        for j in range(i, known, GROUP):
            left = list(range(i, i + GROUP))
            right = list(range(j, j + GROUP))
            products(
                [(quick, k) for k in left], [(quick, k) for k in right], acc_q, right, left,
                (lambda a, b, left=left, right=right: (right[b], left[a])) if i != j else None,
            )
    share_start(slots_q, "slab", slab, slabs, sum_send.at[0], sum_recv.at[0], collapse(acc_q, known, known))

    loads[0].wait()
    loads[1].wait()
    for way in range(2):
        guarded(can_recv[way], lambda way=way: mod_copy(way).wait_recv())

    def coefficients(z, carry):
        for start in range(0, height, rows):
            here = pl.ds(start, rows)
            m = mod[z + 1, pl.ds(PAD + start, rows), :]
            base = (3.4 * m + neighbour_sum(mod, (), z + 1, start, rows)) * 0.0625 - 1.0
            for c in range(3):
                diag[c, z, here, :] = base + 0.125 * ten[c, z, here, :]
        return carry

    lax.fori_loop(0, depth, coefficients, 0)

    def apply(stage, r, c):
        v, g = ((v0, g0), (v1, g1))[stage]
        others = [k for k in range(3) if k != c]
        couple = [3 + c + k - 1 for k in others]

        def body(z, carry):
            for start in range(0, height, rows):
                here = pl.ds(start, rows)
                inner = pl.ds(PAD + start, rows)
                m = mod[z + 1, inner, :]
                out = diag[c, z, here, :] * v[r, c, z + 1, inner, :]
                for k, e in zip(others, couple):
                    out = out + (0.125 * ten[e, z, here, :]) * v[r, k, z + 1, inner, :]
                near = m * neighbour_sum(v, (r, c), z + 1, start, rows) + neighbour_sum(
                    g, (r, c), z + 1, start, rows
                )
                out = out - 0.0625 * near
                if stage == 0:
                    v1[r, c, z + 1, inner, :] = out
                    g1[r, c, z + 1, inner, :] = m * out
                else:
                    filt[r, c * depth + z, here, :] = 2.0 * out - v0[r, c, z + 1, inner, :]
            return carry

        lax.fori_loop(0, depth, body, 0)

    def wait_halo(stage, r, c):
        v, g = ((v0, g0), (v1, g1))[stage]
        for way in range(2):
            guarded(can_recv[way], lambda way=way: halo_copy(stage, r, c, way).wait_recv())
            plane = lands[way]
            g[r, c, plane] = mod[plane] * v[r, c, plane]

    order = sorted(range(1, groups), key=lambda o: (abs(o - groups // 2), o))

    def there_copy(r, c, o):
        to = lax.rem(group + o, groups)
        part = pl.ds(c * depth, depth)
        return pltpu.make_async_remote_copy(
            src_ref=filt.at[r, part, pl.ds(pl.multiple_of(to * share, share), share), :],
            dst_ref=every.at[group * mine + r, part],
            send_sem=there_send.at[r, c, o],
            recv_sem=there_recv.at[r, c, o],
            device_id={"probe": to},
            device_id_type=MESH,
        )

    own_rows = pl.ds(pl.multiple_of(group * share, share), share)

    def keep_copy(r):
        return pltpu.make_async_copy(filt.at[r, :, own_rows, :], every.at[group * mine + r], own_sem.at[r])

    for r in range(mine):
        loads[3 + r].wait()
        for c in range(3):
            for z in range(1, depth + 1):
                g0[r, c, z] = mod[z] * v0[r, c, z]
                blank = jnp.zeros((PAD, LANES), jnp.float32)
                g1[r, c, z, pl.ds(0, PAD), :] = blank
                g1[r, c, z, pl.ds(PAD + height, PAD), :] = blank
        for c in range(3):
            wait_halo(0, r, c)
            apply(0, r, c)
            for way in range(2):
                guarded(can_send[way], lambda way=way, r=r, c=c: halo_copy(1, r, c, way).start())
        if r + 1 < mine:
            send_probe(r + 1)
        if r == 0:
            partial = share_finish(slots_q, "slab", slab, slabs, sum_send.at[0], sum_recv.at[0])
            share_start(slots_qp, "probe", group, groups, sump_send.at[0], sump_recv.at[0], partial)
        for c in range(3):
            wait_halo(1, r, c)
            apply(1, r, c)
            for o in order:
                there_copy(r, c, o).start()
        keep_copy(r).start()

    gram_q = share_finish(slots_qp, "probe", group, groups, sump_send.at[0], sump_recv.at[0])
    square = (known, LANES)
    lane = lax.broadcasted_iota(jnp.int32, square, 1)
    line = lax.broadcasted_iota(jnp.int32, square, 0)
    table = jnp.where(lane < known, gram_q, 0.0) + jnp.where(lane == line + known, 1.0, 0.0)
    for k in range(known):
        column = spread(table[:, k : k + 1], square)
        pivot = spread(column[k : k + 1, :], square)
        lead = spread(table[k : k + 1, :], square) / pivot
        table = jnp.where(line == k, lead, table - column * lead)
    inverse[...] = pltpu.roll(table, LANES - known, 1)
    inv = jnp.where(lane < known, inverse[...], 0.0)
    inverse[...] = inv

    def batch(r):
        ids = [p * mine + r for p in range(groups)]
        return [ids[i : i + GROUP] for i in range(0, groups, GROUP)]

    for r in range(mine):
        keep_copy(r).wait()
        for c in range(3):
            for o in order:
                there_copy(r, c, o).wait_recv()
        for ids in batch(r):
            for i in range(0, known, GROUP):
                left = list(range(i, i + GROUP))
                products([(quick, k) for k in left], [(every, k) for k in ids], acc_y, ids, left, None)
            for before in range(r + 1):
                for old in batch(before):
                    if before == r and old[0] > ids[0]:
                        continue
                    same = old == ids
                    products(
                        [(every, k) for k in old], [(every, k) for k in ids], acc_y, ids,
                        [known + k for k in old],
                        None if same else (lambda a, b, old=old, ids=ids: (known + ids[b], old[a])),
                    )
    part = collapse(acc_y, known + total, total)
    share_start(slots_y, "slab", slab, slabs, sum_send.at[1], sum_recv.at[1], part)
    part = share_finish(slots_y, "slab", slab, slabs, sum_send.at[1], sum_recv.at[1])
    share_start(slots_yp, "probe", group, groups, sump_send.at[1], sump_recv.at[1], part)
    gram_y = share_finish(slots_yp, "probe", group, groups, sump_send.at[1], sump_recv.at[1])

    flat = (total, LANES)
    lane = lax.broadcasted_iota(jnp.int32, flat, 1)
    line = lax.broadcasted_iota(jnp.int32, flat, 0)
    cross = jnp.where(lane < known, gram_y, 0.0)
    coeff = jnp.zeros(flat, jnp.float32)
    for k in range(known):
        coeff = coeff + spread(cross[:, k : k + 1], flat) * spread(inverse[k : k + 1, :], flat)
    nt = (((1,), (1,)), ((), ()))
    taken = lax.dot_general(
        coeff, jnp.concatenate([cross, jnp.zeros((LANES - total, LANES), jnp.float32)], axis=0), nt,
        precision=lax.Precision.HIGHEST, preferred_element_type=jnp.float32,
    )
    at = known + total
    gram = pltpu.roll(gram_y, LANES - known, 1) - taken
    gram = jnp.where(lane < total, gram, 0.0)
    work = pltpu.roll(gram, at, 1) + jnp.where(lane == line + known, 1.0, 0.0) - coeff
    factor = jnp.ones(flat, jnp.float32)
    for k in range(total):
        column = spread(work[:, at + k : at + k + 1], flat)
        pivot = spread(column[k : k + 1, :], flat)
        lead = spread(work[k : k + 1, :], flat) / pivot
        factor = jnp.where(line == k, pivot, factor)
        work = jnp.where(line > k, work - column * lead, work)
    mixing[...] = work * (scale / jnp.sqrt(factor))

    def make(i):
        weights = mixing[pl.ds(i, 1), :]
        splats = [spread(weights[:, v : v + 1], (8, LANES)) for v in range(known + total)]

        def step(f, carry):
            for t in range(share // 8):
                sub = pl.ds(8 * t, 8)
                value = splats[0] * quick[0, f, sub, :]
                for v in range(1, known):
                    value = value + splats[v] * quick[v, f, sub, :]
                for v in range(total):
                    value = value + splats[known + v] * every[v, f, sub, :]
                outgoing[i, f, sub, :] = value
            return carry

        lax.fori_loop(0, fields, step, 0)

    def back_copy(r, o):
        to = lax.rem(group + o, groups)
        return pltpu.make_async_remote_copy(
            src_ref=outgoing.at[to * mine + r],
            dst_ref=basis_ref.at[r, :, own_rows, :],
            send_sem=back_send.at[r, o],
            recv_sem=back_recv.at[r, o],
            device_id={"probe": to},
            device_id_type=MESH,
        )

    def own_copy(r):
        return pltpu.make_async_copy(
            outgoing.at[group * mine + r], basis_ref.at[r, :, own_rows, :], own_sem.at[mine + r]
        )

    for o in order:
        for r in range(mine):
            make(lax.rem(group + o, groups) * mine + r)
            back_copy(r, o).start()
    for r in range(mine):
        make(group * mine + r)
        own_copy(r).start()

    corr_ref[...] = coeff[:, :known] * scale

    for way in range(2):
        def finish(way=way):
            mod_copy(way).wait_send()
            for stage in range(2):
                for r in range(mine):
                    for c in range(3):
                        halo_copy(stage, r, c, way).wait_send()
        guarded(can_send[way], finish)
    for r in range(mine):
        own_copy(r).wait()
        for o in order:
            for c in range(3):
                there_copy(r, c, o).wait_send()
            back_copy(r, o).wait()


def body(probes, earlier, modulus, tangent):
    mine, parts, depth, height, width = probes.shape
    known, _, _, share, _ = earlier.shape
    slabs = lax.axis_size("slab")
    groups = lax.axis_size("probe")
    total = mine * groups
    fields = parts * depth
    scale = float(parts * depth * slabs * height * width) ** 0.5
    f32 = jnp.float32
    padded = (mine, parts, depth + 2, height + 2 * PAD, width)
    dma = pltpu.SemaphoreType.DMA
    anywhere = pl.BlockSpec(memory_space=pltpu.HBM)
    basis, corr = pl.pallas_call(
        functools.partial(kernel, slabs, groups, scale),
        out_shape=(
            jax.ShapeDtypeStruct((mine, fields, height, width), f32),
            jax.ShapeDtypeStruct((total, known), f32),
        ),
        in_specs=[anywhere] * 4,
        out_specs=(anywhere, pl.BlockSpec(memory_space=pltpu.VMEM)),
        scratch_shapes=[
            pltpu.VMEM(padded, f32),
            pltpu.VMEM(padded, f32),
            pltpu.VMEM(padded, f32),
            pltpu.VMEM(padded, f32),
            pltpu.VMEM((depth + 2, height + 2 * PAD, width), f32),
            pltpu.VMEM((6, depth, height, width), f32),
            pltpu.VMEM((3, depth, height, width), f32),
            pltpu.VMEM((known, fields, share, width), f32),
            pltpu.VMEM((mine, fields, height, width), f32),
            pltpu.VMEM((total, fields, share, width), f32),
            pltpu.VMEM((total, fields, share, width), f32),
            pltpu.VMEM((known, known, 8, width), f32),
            pltpu.VMEM((known + total, total, 8, width), f32),
            pltpu.VMEM((slabs, known, LANES), f32),
            pltpu.VMEM((groups, known, LANES), f32),
            pltpu.VMEM((slabs, total, LANES), f32),
            pltpu.VMEM((groups, total, LANES), f32),
            pltpu.VMEM((known, LANES), f32),
            pltpu.VMEM((total, LANES), f32),
            dma((3 + mine,)),
            dma((2, mine, parts, 2)),
            dma((2, mine, parts, 2)),
            dma((2,)),
            dma((2,)),
            dma((mine, parts, groups)),
            dma((mine, parts, groups)),
            dma((mine, groups)),
            dma((mine, groups)),
            dma((2, slabs)),
            dma((2, slabs)),
            dma((2, groups)),
            dma((2, groups)),
            dma((2 * mine,)),
        ],
        compiler_params=pltpu.CompilerParams(
            collective_id=0, has_side_effects=True, vmem_limit_bytes=60 * 1024 * 1024
        ),
    )(probes, earlier.reshape(known, fields, share, width), modulus, tangent)
    return basis.reshape(probes.shape), corr.T


def solution(mesh):
    in_specs = (
        P("probe", None, "slab", None, None),
        P(None, None, "slab", "probe", None),
        P("slab", None, None),
        P(None, "slab", None, None),
    )
    out_specs = (P("probe", None, "slab", None, None), P())
    return jax.shard_map(body, mesh=mesh, in_specs=in_specs, out_specs=out_specs, check_vma=False)
```

```python
import functools

import jax
import jax.numpy as jnp
from jax import lax
from jax.experimental import pallas as pl
from jax.experimental.pallas import tpu as pltpu
from jax.sharding import PartitionSpec as P

MESH = pl.DeviceIdType.MESH
LANES = 128
PAD = 8
GROUP = 4


def neighbour_sum(ref, lead, z, start, rows):
    def at(plane, off):
        return ref[lead + (plane, pl.ds(PAD + start + off, rows), slice(None))]

    centre = at(z, 0)
    beside = at(z, -1) + at(z, 1)
    above = at(z - 1, 0) + at(z + 1, 0)
    corner = (at(z - 1, -1) + at(z + 1, -1)) + (at(z - 1, 1) + at(z + 1, 1))
    along = 0.3 * centre + 0.1 * (above + beside) + 0.05 * corner
    still = 0.3 * (above + beside) + 0.1 * corner
    width = along.shape[-1]
    lane = lax.broadcasted_iota(jnp.int32, along.shape, 1)
    from_left = jnp.where(lane == 0, 0.0, pltpu.roll(along, 1, 1))
    from_right = jnp.where(lane == width - 1, 0.0, pltpu.roll(along, width - 1, 1))
    return still + from_left + from_right


def spread(column, shape):
    return jnp.broadcast_to(column, shape)


def kernel(
    slabs, groups,
    probes_ref, earlier_ref, modulus_ref, tangent_ref,
    basis_ref, corr_ref,
    v0, v1, g0, g1, mod, ten, diag, quick, filt, every, outgoing,
    acc_q, acc_y, slots_q, slots_qp, slots_y, slots_yp, inverse, mixing,
    load_sem, halo_send, halo_recv, mod_send, mod_recv,
    there_send, there_recv, back_send, back_recv,
    sum_send, sum_recv, sump_send, sump_recv, own_sem,
):
    slab = lax.axis_index("slab")
    group = lax.axis_index("probe")
    mine, _, depth, height, _ = probes_ref.shape
    known, fields, share, _ = earlier_ref.shape
    total = mine * groups
    rows = 32

    loads = [
        pltpu.make_async_copy(modulus_ref, mod.at[pl.ds(1, depth), pl.ds(PAD, height), :], load_sem.at[0]),
        pltpu.make_async_copy(tangent_ref, ten, load_sem.at[1]),
        pltpu.make_async_copy(earlier_ref, quick, load_sem.at[2]),
    ]
    for r in range(mine):
        loads.append(
            pltpu.make_async_copy(
                probes_ref.at[r],
                v0.at[r, :, pl.ds(1, depth), pl.ds(PAD, height), :],
                load_sem.at[3 + r],
            )
        )
    for i in [0] + list(range(3, 3 + mine)) + [1, 2]:
        loads[i].start()

    barrier = pltpu.get_barrier_semaphore()
    for o in range(1, slabs):
        pl.semaphore_signal(barrier, inc=1, device_id={"slab": lax.rem(slab + o, slabs)}, device_id_type=MESH)
    for o in range(1, groups):
        pl.semaphore_signal(barrier, inc=1, device_id={"probe": lax.rem(group + o, groups)}, device_id_type=MESH)

    for ref in (v0, v1):
        edge = jnp.zeros(ref.shape[:3] + (PAD, LANES), jnp.float32)
        ref[:, :, :, pl.ds(0, PAD), :] = edge
        ref[:, :, :, pl.ds(PAD + height, PAD), :] = edge
    edge = jnp.zeros((depth + 2, PAD, LANES), jnp.float32)
    mod[:, pl.ds(0, PAD), :] = edge
    mod[:, pl.ds(PAD + height, PAD), :] = edge

    def clear(plane):
        for ref in (v0, v1):
            ref[:, :, plane, pl.ds(PAD, height), :] = jnp.zeros((mine, 3, height, LANES), jnp.float32)
        mod[plane, pl.ds(PAD, height), :] = jnp.zeros((height, LANES), jnp.float32)

    @pl.when(slab == 0)
    def _():
        clear(0)

    @pl.when(slab == slabs - 1)
    def _():
        clear(depth + 1)

    pl.semaphore_wait(barrier, slabs + groups - 2)

    towards = (lax.rem(slab + slabs - 1, slabs), lax.rem(slab + 1, slabs))
    can_send = (slab > 0, slab < slabs - 1)
    can_recv = (slab < slabs - 1, slab > 0)
    lands = (depth + 1, 0)

    def mod_copy(way):
        return pltpu.make_async_remote_copy(
            src_ref=modulus_ref.at[(0, depth - 1)[way]],
            dst_ref=mod.at[lands[way], pl.ds(PAD, height), :],
            send_sem=mod_send.at[way],
            recv_sem=mod_recv.at[way],
            device_id={"slab": towards[way]},
            device_id_type=MESH,
        )

    def halo_copy(stage, r, c, way):
        if stage == 0:
            source, into = probes_ref.at[r, c, (0, depth - 1)[way]], v0
        else:
            source, into = v1.at[r, c, (1, depth)[way], pl.ds(PAD, height), :], v1
        return pltpu.make_async_remote_copy(
            src_ref=source,
            dst_ref=into.at[r, c, lands[way], pl.ds(PAD, height), :],
            send_sem=halo_send.at[stage, r, c, way],
            recv_sem=halo_recv.at[stage, r, c, way],
            device_id={"slab": towards[way]},
            device_id_type=MESH,
        )

    def guarded(condition, act):
        @pl.when(condition)
        def _():
            act()

    def send_probe(r):
        for way in range(2):
            def begin(way=way):
                if r == 0:
                    mod_copy(way).start()
                for c in range(3):
                    halo_copy(0, r, c, way).start()
            guarded(can_send[way], begin)

    send_probe(0)

    def products(first, second, acc_ref, rows_at, cols_at, mirror_at, begin, end, fresh):
        def step(f, accs):
            left = [ref[k, f] for ref, k in first]
            right = [ref[k, f] for ref, k in second]
            out = []
            n = 0
            for a in left:
                for b in right:
                    prod = a * b
                    part = accs[n]
                    for t in range(share // 8):
                        part = part + prod[8 * t : 8 * t + 8]
                    out.append(part)
                    n += 1
            return tuple(out)

        zero = jnp.zeros((8, LANES), jnp.float32)
        if fresh:
            accs = (zero,) * (len(first) * len(second))
        else:
            accs = tuple(acc_ref[col, row] for col in cols_at for row in rows_at)
        accs = lax.fori_loop(begin, end, step, accs)
        n = 0
        for i in range(len(first)):
            for j in range(len(second)):
                acc_ref[cols_at[i], rows_at[j]] = accs[n]
                if mirror_at is not None:
                    col, row = mirror_at(i, j)
                    acc_ref[col, row] = accs[n]
                n += 1

    def collapse(acc_ref, cols, count):
        lane = lax.broadcasted_iota(jnp.int32, (count, LANES), 1)
        result = jnp.zeros((count, LANES), jnp.float32)
        for v in range(cols):
            summed = jnp.sum(jnp.sum(acc_ref[v], axis=1), axis=1, keepdims=True)
            result = jnp.where(lane == v, spread(summed, (count, LANES)), result)
        return result

    def share_copy(slots, axis, me, count, o, sends, recvs):
        return pltpu.make_async_remote_copy(
            src_ref=slots.at[me],
            dst_ref=slots.at[me],
            send_sem=sends.at[o],
            recv_sem=recvs.at[o],
            device_id={axis: lax.rem(me + o, count)},
            device_id_type=MESH,
        )

    def share_start(slots, axis, me, count, sends, recvs, value):
        slots[me] = value
        for o in range(1, count):
            share_copy(slots, axis, me, count, o, sends, recvs).start()

    def share_finish(slots, axis, me, count, sends, recvs):
        for o in range(1, count):
            share_copy(slots, axis, me, count, o, sends, recvs).wait()
        value = slots[0]
        for i in range(1, count):
            value = value + slots[i]
        return value

    loads[0].wait()
    loads[1].wait()
    for way in range(2):
        guarded(can_recv[way], lambda way=way: mod_copy(way).wait_recv())

    def coefficients(z, carry):
        for start in range(0, height, rows):
            here = pl.ds(start, rows)
            m = mod[z + 1, pl.ds(PAD + start, rows), :]
            base = (3.4 * m + neighbour_sum(mod, (), z + 1, start, rows)) * 0.0625 - 1.0
            for c in range(3):
                diag[c, z, here, :] = base + 0.125 * ten[c, z, here, :]
        return carry

    lax.fori_loop(0, depth, coefficients, 0)

    def apply(stage, r, c):
        v, g = ((v0, g0), (v1, g1))[stage]
        others = [k for k in range(3) if k != c]
        couple = [3 + c + k - 1 for k in others]

        def body(z, carry):
            for start in range(0, height, rows):
                here = pl.ds(start, rows)
                inner = pl.ds(PAD + start, rows)
                m = mod[z + 1, inner, :]
                out = diag[c, z, here, :] * v[r, c, z + 1, inner, :]
                for k, e in zip(others, couple):
                    out = out + (0.125 * ten[e, z, here, :]) * v[r, k, z + 1, inner, :]
                near = m * neighbour_sum(v, (r, c), z + 1, start, rows) + neighbour_sum(
                    g, (r, c), z + 1, start, rows
                )
                out = out - 0.0625 * near
                if stage == 0:
                    v1[r, c, z + 1, inner, :] = out
                    g1[r, c, z + 1, inner, :] = m * out
                else:
                    filt[r, c * depth + z, here, :] = 2.0 * out - v0[r, c, z + 1, inner, :]
            return carry

        lax.fori_loop(0, depth, body, 0)

    def wait_halo(stage, r, c):
        v, g = ((v0, g0), (v1, g1))[stage]
        for way in range(2):
            guarded(can_recv[way], lambda way=way: halo_copy(stage, r, c, way).wait_recv())
            plane = lands[way]
            g[r, c, plane] = mod[plane] * v[r, c, plane]

    order = sorted(range(1, groups), key=lambda o: (abs(o - groups // 2), o))

    def there_copy(r, c, o):
        to = lax.rem(group + o, groups)
        part = pl.ds(c * depth, depth)
        return pltpu.make_async_remote_copy(
            src_ref=filt.at[r, part, pl.ds(pl.multiple_of(to * share, share), share), :],
            dst_ref=every.at[group * mine + r, part],
            send_sem=there_send.at[r, c, o],
            recv_sem=there_recv.at[r, c, o],
            device_id={"probe": to},
            device_id_type=MESH,
        )

    own_rows = pl.ds(pl.multiple_of(group * share, share), share)

    def keep_copy(r):
        return pltpu.make_async_copy(filt.at[r, :, own_rows, :], every.at[group * mine + r], own_sem.at[r])

    for r in range(mine):
        loads[3 + r].wait()
        for c in range(3):
            for z in range(1, depth + 1):
                g0[r, c, z] = mod[z] * v0[r, c, z]
                blank = jnp.zeros((PAD, LANES), jnp.float32)
                g1[r, c, z, pl.ds(0, PAD), :] = blank
                g1[r, c, z, pl.ds(PAD + height, PAD), :] = blank
        for c in range(3):
            wait_halo(0, r, c)
            apply(0, r, c)
            for way in range(2):
                guarded(can_send[way], lambda way=way, r=r, c=c: halo_copy(1, r, c, way).start())
        if r + 1 < mine:
            send_probe(r + 1)
        if r == 0:
            loads[2].wait()
            for i in range(0, known, GROUP):
                for j in range(i, known, GROUP):
                    left = list(range(i, i + GROUP))
                    right = list(range(j, j + GROUP))
                    products(
                        [(quick, k) for k in left], [(quick, k) for k in right], acc_q, right, left,
                        (lambda a, b, left=left, right=right: (right[b], left[a])) if i != j else None,
                        0, fields, True,
                    )
            share_start(slots_q, "slab", slab, slabs, sum_send.at[0], sum_recv.at[0], collapse(acc_q, known, known))
        if r == mine - 1:
            partial = share_finish(slots_q, "slab", slab, slabs, sum_send.at[0], sum_recv.at[0])
            share_start(slots_qp, "probe", group, groups, sump_send.at[0], sump_recv.at[0], partial)
        for c in range(3):
            wait_halo(1, r, c)
            apply(1, r, c)
            for o in order:
                there_copy(r, c, o).start()
        keep_copy(r).start()

    gram_q = share_finish(slots_qp, "probe", group, groups, sump_send.at[0], sump_recv.at[0])
    square = (known, LANES)
    lane = lax.broadcasted_iota(jnp.int32, square, 1)
    line = lax.broadcasted_iota(jnp.int32, square, 0)
    table = jnp.where(lane < known, gram_q, 0.0) + jnp.where(lane == line + known, 1.0, 0.0)
    for k in range(known):
        column = spread(table[:, k : k + 1], square)
        pivot = spread(column[k : k + 1, :], square)
        lead = spread(table[k : k + 1, :], square) / pivot
        table = jnp.where(line == k, lead, table - column * lead)
    inverse[...] = pltpu.roll(table, LANES - known, 1)
    inv = jnp.where(lane < known, inverse[...], 0.0)
    inverse[...] = inv

    def batch(r):
        ids = [p * mine + r for p in range(groups)]
        return [ids[i : i + GROUP] for i in range(0, groups, GROUP)]

    for r in range(mine):
        keep_copy(r).wait()
        for c in range(3):
            for o in order:
                there_copy(r, c, o).wait_recv()
            span = (c * depth, (c + 1) * depth, c == 0)
            for ids in batch(r):
                for i in range(0, known, GROUP):
                    left = list(range(i, i + GROUP))
                    products([(quick, k) for k in left], [(every, k) for k in ids], acc_y, ids, left, None, *span)
                for before in range(r + 1):
                    for old in batch(before):
                        if before == r and old[0] > ids[0]:
                            continue
                        same = old == ids
                        products(
                            [(every, k) for k in old], [(every, k) for k in ids], acc_y, ids,
                            [known + k for k in old],
                            None if same else (lambda a, b, old=old, ids=ids: (known + ids[b], old[a])),
                            *span,
                        )
    part = collapse(acc_y, known + total, total)
    share_start(slots_y, "slab", slab, slabs, sum_send.at[1], sum_recv.at[1], part)
    part = share_finish(slots_y, "slab", slab, slabs, sum_send.at[1], sum_recv.at[1])
    share_start(slots_yp, "probe", group, groups, sump_send.at[1], sump_recv.at[1], part)
    gram_y = share_finish(slots_yp, "probe", group, groups, sump_send.at[1], sump_recv.at[1])

    flat = (total, LANES)
    lane = lax.broadcasted_iota(jnp.int32, flat, 1)
    line = lax.broadcasted_iota(jnp.int32, flat, 0)
    cross = jnp.where(lane < known, gram_y, 0.0)
    coeff = jnp.zeros(flat, jnp.float32)
    for k in range(known):
        coeff = coeff + spread(cross[:, k : k + 1], flat) * spread(inverse[k : k + 1, :], flat)
    nt = (((1,), (1,)), ((), ()))
    taken = lax.dot_general(
        coeff, jnp.concatenate([cross, jnp.zeros((LANES - total, LANES), jnp.float32)], axis=0), nt,
        precision=lax.Precision.HIGHEST, preferred_element_type=jnp.float32,
    )
    at = known + total
    gram = pltpu.roll(gram_y, LANES - known, 1) - taken
    gram = jnp.where(lane < total, gram, 0.0)
    work = pltpu.roll(gram, at, 1) + jnp.where(lane == line + known, 1.0, 0.0) - coeff
    factor = jnp.ones(flat, jnp.float32)
    for k in range(total):
        column = spread(work[:, at + k : at + k + 1], flat)
        pivot = spread(column[k : k + 1, :], flat)
        lead = spread(work[k : k + 1, :], flat) / pivot
        factor = jnp.where(line == k, pivot, factor)
        work = jnp.where(line > k, work - column * lead, work)
    mixing[...] = work / jnp.sqrt(factor)

    def make(i):
        weights = mixing[pl.ds(i, 1), :]
        splats = [spread(weights[:, v : v + 1], (8, LANES)) for v in range(known + total)]

        def step(f, carry):
            for t in range(share // 8):
                sub = pl.ds(8 * t, 8)
                value = splats[0] * quick[0, f, sub, :]
                for v in range(1, known):
                    value = value + splats[v] * quick[v, f, sub, :]
                for v in range(total):
                    value = value + splats[known + v] * every[v, f, sub, :]
                outgoing[i, f, sub, :] = value
            return carry

        lax.fori_loop(0, fields, step, 0)

    def back_copy(r, o):
        to = lax.rem(group + o, groups)
        return pltpu.make_async_remote_copy(
            src_ref=outgoing.at[to * mine + r],
            dst_ref=basis_ref.at[r, :, own_rows, :],
            send_sem=back_send.at[r, o],
            recv_sem=back_recv.at[r, o],
            device_id={"probe": to},
            device_id_type=MESH,
        )

    def own_copy(r):
        return pltpu.make_async_copy(
            outgoing.at[group * mine + r], basis_ref.at[r, :, own_rows, :], own_sem.at[mine + r]
        )

    for o in order:
        for r in range(mine):
            make(lax.rem(group + o, groups) * mine + r)
            back_copy(r, o).start()
    for r in range(mine):
        make(group * mine + r)
        own_copy(r).start()

    corr_ref[...] = coeff[:, :known]

    for way in range(2):
        def finish(way=way):
            mod_copy(way).wait_send()
            for stage in range(2):
                for r in range(mine):
                    for c in range(3):
                        halo_copy(stage, r, c, way).wait_send()
        guarded(can_send[way], finish)
    for r in range(mine):
        own_copy(r).wait()
        for o in order:
            for c in range(3):
                there_copy(r, c, o).wait_send()
            back_copy(r, o).wait()


def body(probes, earlier, modulus, tangent):
    mine, parts, depth, height, width = probes.shape
    known, _, _, share, _ = earlier.shape
    slabs = lax.axis_size("slab")
    groups = lax.axis_size("probe")
    total = mine * groups
    fields = parts * depth
    scale = float(parts * depth * slabs * height * width) ** 0.5
    f32 = jnp.float32
    padded = (mine, parts, depth + 2, height + 2 * PAD, width)
    dma = pltpu.SemaphoreType.DMA
    anywhere = pl.BlockSpec(memory_space=pltpu.HBM)
    basis, corr = pl.pallas_call(
        functools.partial(kernel, slabs, groups),
        out_shape=(
            jax.ShapeDtypeStruct((mine, fields, height, width), f32),
            jax.ShapeDtypeStruct((total, known), f32),
        ),
        in_specs=[anywhere] * 4,
        out_specs=(anywhere, pl.BlockSpec(memory_space=pltpu.VMEM)),
        scratch_shapes=[
            pltpu.VMEM(padded, f32),
            pltpu.VMEM(padded, f32),
            pltpu.VMEM(padded, f32),
            pltpu.VMEM(padded, f32),
            pltpu.VMEM((depth + 2, height + 2 * PAD, width), f32),
            pltpu.VMEM((6, depth, height, width), f32),
            pltpu.VMEM((3, depth, height, width), f32),
            pltpu.VMEM((known, fields, share, width), f32),
            pltpu.VMEM((mine, fields, height, width), f32),
            pltpu.VMEM((total, fields, share, width), f32),
            pltpu.VMEM((total, fields, share, width), f32),
            pltpu.VMEM((known, known, 8, width), f32),
            pltpu.VMEM((known + total, total, 8, width), f32),
            pltpu.VMEM((slabs, known, LANES), f32),
            pltpu.VMEM((groups, known, LANES), f32),
            pltpu.VMEM((slabs, total, LANES), f32),
            pltpu.VMEM((groups, total, LANES), f32),
            pltpu.VMEM((known, LANES), f32),
            pltpu.VMEM((total, LANES), f32),
            dma((3 + mine,)),
            dma((2, mine, parts, 2)),
            dma((2, mine, parts, 2)),
            dma((2,)),
            dma((2,)),
            dma((mine, parts, groups)),
            dma((mine, parts, groups)),
            dma((mine, groups)),
            dma((mine, groups)),
            dma((2, slabs)),
            dma((2, slabs)),
            dma((2, groups)),
            dma((2, groups)),
            dma((2 * mine,)),
        ],
        compiler_params=pltpu.CompilerParams(
            collective_id=0, has_side_effects=True, vmem_limit_bytes=60 * 1024 * 1024
        ),
    )(probes, earlier.reshape(known, fields, share, width), modulus, tangent)
    return basis.reshape(probes.shape) * scale, corr.T * scale


def solution(mesh):
    in_specs = (
        P("probe", None, "slab", None, None),
        P(None, None, "slab", "probe", None),
        P("slab", None, None),
        P(None, "slab", None, None),
    )
    out_specs = (P("probe", None, "slab", None, None), P())
    return jax.shard_map(body, mesh=mesh, in_specs=in_specs, out_specs=out_specs, check_vma=False)
```

```python
import functools

import jax
import jax.numpy as jnp
from jax import lax
from jax.experimental import pallas as pl
from jax.experimental.pallas import tpu as pltpu
from jax.sharding import PartitionSpec as P

MESH = pl.DeviceIdType.MESH
LANES = 128
PAD = 8
GROUP = 4
EDGE = 2


def neighbour_sum(ref, lead, z, start, rows):
    def at(plane, off):
        return ref[lead + (plane, pl.ds(PAD + start + off, rows), slice(None))]

    centre = at(z, 0)
    beside = at(z, -1) + at(z, 1)
    above = at(z - 1, 0) + at(z + 1, 0)
    corner = (at(z - 1, -1) + at(z + 1, -1)) + (at(z - 1, 1) + at(z + 1, 1))
    along = 0.3 * centre + 0.1 * (above + beside) + 0.05 * corner
    still = 0.3 * (above + beside) + 0.1 * corner
    width = along.shape[-1]
    lane = lax.broadcasted_iota(jnp.int32, along.shape, 1)
    from_left = jnp.where(lane == 0, 0.0, pltpu.roll(along, 1, 1))
    from_right = jnp.where(lane == width - 1, 0.0, pltpu.roll(along, width - 1, 1))
    return still + from_left + from_right


def spread(column, shape):
    return jnp.broadcast_to(column, shape)


def kernel(
    slabs, groups,
    probes_ref, earlier_ref, modulus_ref, tangent_ref,
    basis_ref, corr_ref,
    v0, v1, g0, g1, t0, t1, h0, h1, mod, ten, diag, tmod, tten, tdiag, quick, filt, every, outgoing,
    acc_q, acc_y, slots_q, slots_qp, slots_y, slots_yp, inverse, mixing,
    load_sem, halo_send, halo_recv, mod_send, mod_recv,
    there_send, there_recv, back_send, back_recv,
    sum_send, sum_recv, sump_send, sump_recv, own_sem,
    raw_send, raw_recv, raw_own, quarter_send, quarter_recv,
):
    slab = lax.axis_index("slab")
    group = lax.axis_index("probe")
    mine, _, depth, height, _ = probes_ref.shape
    known, fields, share, _ = earlier_ref.shape
    total = mine * groups
    rows = 32
    first = mine - 1
    wide = share + 2 * PAD

    loads = [
        pltpu.make_async_copy(modulus_ref, mod.at[pl.ds(1, depth), pl.ds(PAD, height), :], load_sem.at[0]),
        pltpu.make_async_copy(tangent_ref, ten.at[:, :, pl.ds(PAD, height), :], load_sem.at[1]),
        pltpu.make_async_copy(earlier_ref, quick, load_sem.at[2]),
    ]
    for r in range(first):
        loads.append(
            pltpu.make_async_copy(
                probes_ref.at[r],
                v0.at[r, :, pl.ds(1, depth), pl.ds(PAD, height), :],
                load_sem.at[3 + r],
            )
        )
    for i in [0] + list(range(3, 3 + first)) + [1, 2]:
        loads[i].start()

    barrier = pltpu.get_barrier_semaphore()
    for o in range(1, slabs):
        pl.semaphore_signal(barrier, inc=1, device_id={"slab": lax.rem(slab + o, slabs)}, device_id_type=MESH)
    for o in range(1, groups):
        pl.semaphore_signal(barrier, inc=1, device_id={"probe": lax.rem(group + o, groups)}, device_id_type=MESH)

    for ref in (v0, v1):
        edge = jnp.zeros(ref.shape[:3] + (PAD, LANES), jnp.float32)
        ref[:, :, :, pl.ds(0, PAD), :] = edge
        ref[:, :, :, pl.ds(PAD + height, PAD), :] = edge
    for ref in (ten, diag):
        edge = jnp.zeros(ref.shape[:2] + (PAD, LANES), jnp.float32)
        ref[:, :, pl.ds(0, PAD), :] = edge
        ref[:, :, pl.ds(PAD + height, PAD), :] = edge
    for ref in (t0, t1):
        edge = jnp.zeros(ref.shape[:3] + (PAD - EDGE, LANES), jnp.float32)
        ref[:, :, :, pl.ds(0, PAD - EDGE), :] = edge
        ref[:, :, :, pl.ds(PAD + share + EDGE, PAD - EDGE), :] = edge
    edge = jnp.zeros((depth + 2, PAD, LANES), jnp.float32)
    mod[:, pl.ds(0, PAD), :] = edge
    mod[:, pl.ds(PAD + height, PAD), :] = edge

    def clear(plane):
        for ref in (v0, v1):
            ref[:, :, plane, pl.ds(PAD, height), :] = jnp.zeros((first, 3, height, LANES), jnp.float32)
        for ref in (t0, t1):
            ref[:, :, plane] = jnp.zeros((groups, 3, wide, LANES), jnp.float32)
        mod[plane, pl.ds(PAD, height), :] = jnp.zeros((height, LANES), jnp.float32)

    def clear_rows(ref, start):
        count = ref.shape[0]
        blank = jnp.zeros((count, 3, depth, EDGE, LANES), jnp.float32)
        ref[:, :, pl.ds(1, depth), pl.ds(start, EDGE), :] = blank

    @pl.when(group == 0)
    def _():
        clear_rows(t0, PAD - EDGE)

    @pl.when(group == groups - 1)
    def _():
        clear_rows(t0, PAD + share)

    @pl.when(slab == 0)
    def _():
        clear(0)

    @pl.when(slab == slabs - 1)
    def _():
        clear(depth + 1)

    pl.semaphore_wait(barrier, slabs + groups - 2)

    towards = (lax.rem(slab + slabs - 1, slabs), lax.rem(slab + 1, slabs))
    can_send = (slab > 0, slab < slabs - 1)
    can_recv = (slab < slabs - 1, slab > 0)
    lands = (depth + 1, 0)

    def mod_copy(way):
        return pltpu.make_async_remote_copy(
            src_ref=modulus_ref.at[(0, depth - 1)[way]],
            dst_ref=mod.at[lands[way], pl.ds(PAD, height), :],
            send_sem=mod_send.at[way],
            recv_sem=mod_recv.at[way],
            device_id={"slab": towards[way]},
            device_id_type=MESH,
        )

    def halo_copy(stage, r, c, way):
        if stage == 0:
            source, into = probes_ref.at[r, c, (0, depth - 1)[way]], v0
        else:
            source, into = v1.at[r, c, (1, depth)[way], pl.ds(PAD, height), :], v1
        return pltpu.make_async_remote_copy(
            src_ref=source,
            dst_ref=into.at[r, c, lands[way], pl.ds(PAD, height), :],
            send_sem=halo_send.at[stage, r, c, way],
            recv_sem=halo_recv.at[stage, r, c, way],
            device_id={"slab": towards[way]},
            device_id_type=MESH,
        )

    def guarded(condition, act):
        @pl.when(condition)
        def _():
            act()

    def send_probe(r):
        for way in range(2):
            def begin(way=way):
                if r == 0:
                    mod_copy(way).start()
                for c in range(3):
                    halo_copy(0, r, c, way).start()
            guarded(can_send[way], begin)

    def raw_part(kind, to):
        return (
            pl.ds(pl.multiple_of(to * share, share), share),
            pl.ds(to * share - EDGE, EDGE),
            pl.ds(to * share + share, EDGE),
        )[kind]

    raw_rows = (pl.ds(PAD, share), pl.ds(PAD - EDGE, EDGE), pl.ds(PAD + share, EDGE))

    def raw_copy(kind, o, arriving=False):
        to = lax.rem(group + o, groups)
        landing = t0.at[group, :, pl.ds(1, depth), raw_rows[kind], :]
        return pltpu.make_async_remote_copy(
            src_ref=landing if arriving else probes_ref.at[first, :, :, raw_part(kind, to), :],
            dst_ref=t0.at[group, :, pl.ds(1, depth), raw_rows[kind], :],
            send_sem=raw_send.at[kind, o],
            recv_sem=raw_recv.at[kind, o],
            device_id={"probe": to},
            device_id_type=MESH,
        )

    def raw_local(kind):
        return pltpu.make_async_copy(
            probes_ref.at[first, :, :, raw_part(kind, group), :],
            t0.at[group, :, pl.ds(1, depth), raw_rows[kind], :],
            raw_own.at[kind],
        )

    def in_mesh(kind, to):
        return (None, to > 0, to < groups - 1)[kind]

    def maybe(condition, act):
        if condition is None:
            act()
        else:
            guarded(condition, act)

    order = sorted(range(1, groups), key=lambda o: (abs(o - groups // 2), o))

    send_probe(0)
    for kind in range(3):
        maybe(in_mesh(kind, group), lambda kind=kind: raw_local(kind).start())
    for o in order:
        to = lax.rem(group + o, groups)
        for kind in range(3):
            maybe(in_mesh(kind, to), lambda kind=kind, o=o: raw_copy(kind, o).start())

    def quarter_copy(stage, o, way):
        ref = (t0, t1)[stage]
        source = lax.rem(group + groups - o, groups)
        span = pl.ds(PAD - EDGE, share + 2 * EDGE)
        return pltpu.make_async_remote_copy(
            src_ref=ref.at[source, :, (1, depth)[way], span, :],
            dst_ref=ref.at[source, :, lands[way], span, :],
            send_sem=quarter_send.at[stage, o, way],
            recv_sem=quarter_recv.at[stage, o, way],
            device_id={"slab": towards[way]},
            device_id_type=MESH,
        )

    def quarter_send_all(stage, o):
        for way in range(2):
            guarded(can_send[way], lambda way=way: quarter_copy(stage, o, way).start())

    def quarter_wait(stage, o):
        for way in range(2):
            guarded(can_recv[way], lambda way=way: quarter_copy(stage, o, way).wait_recv())

    def products(first, second, acc_ref, rows_at, cols_at, mirror_at, begin, end, fresh):
        def step(f, accs):
            left = [ref[k, f] for ref, k in first]
            right = [ref[k, f] for ref, k in second]
            out = []
            n = 0
            for a in left:
                for b in right:
                    prod = a * b
                    part = accs[n]
                    for t in range(share // 8):
                        part = part + prod[8 * t : 8 * t + 8]
                    out.append(part)
                    n += 1
            return tuple(out)

        zero = jnp.zeros((8, LANES), jnp.float32)
        if fresh:
            accs = (zero,) * (len(first) * len(second))
        else:
            accs = tuple(acc_ref[col, row] for col in cols_at for row in rows_at)
        accs = lax.fori_loop(begin, end, step, accs)
        n = 0
        for i in range(len(first)):
            for j in range(len(second)):
                acc_ref[cols_at[i], rows_at[j]] = accs[n]
                if mirror_at is not None:
                    col, row = mirror_at(i, j)
                    acc_ref[col, row] = accs[n]
                n += 1

    def collapse(acc_ref, cols, count):
        lane = lax.broadcasted_iota(jnp.int32, (count, LANES), 1)
        result = jnp.zeros((count, LANES), jnp.float32)
        for v in range(cols):
            summed = jnp.sum(jnp.sum(acc_ref[v], axis=1), axis=1, keepdims=True)
            result = jnp.where(lane == v, spread(summed, (count, LANES)), result)
        return result

    def share_copy(slots, axis, me, count, o, sends, recvs):
        return pltpu.make_async_remote_copy(
            src_ref=slots.at[me],
            dst_ref=slots.at[me],
            send_sem=sends.at[o],
            recv_sem=recvs.at[o],
            device_id={axis: lax.rem(me + o, count)},
            device_id_type=MESH,
        )

    def share_start(slots, axis, me, count, sends, recvs, value):
        slots[me] = value
        for o in range(1, count):
            share_copy(slots, axis, me, count, o, sends, recvs).start()

    def share_finish(slots, axis, me, count, sends, recvs):
        for o in range(1, count):
            share_copy(slots, axis, me, count, o, sends, recvs).wait()
        value = slots[0]
        for i in range(1, count):
            value = value + slots[i]
        return value

    loads[0].wait()
    loads[1].wait()
    for way in range(2):
        guarded(can_recv[way], lambda way=way: mod_copy(way).wait_recv())

    def coefficients(z, carry):
        for start in range(0, height, rows):
            here = pl.ds(PAD + start, rows)
            m = mod[z + 1, here, :]
            base = (3.4 * m + neighbour_sum(mod, (), z + 1, start, rows)) * 0.0625 - 1.0
            for c in range(3):
                diag[c, z, here, :] = base + 0.125 * ten[c, z, here, :]
        return carry

    lax.fori_loop(0, depth, coefficients, 0)

    def apply(v, g, fields_of, lead, c, chunks, store):
        mods, diags, tens = fields_of
        others = [k for k in range(3) if k != c]
        couple = [3 + c + k - 1 for k in others]

        def body(z, carry):
            for start, size in chunks:
                inner = pl.ds(PAD + start, size)
                m = mods[z + 1, inner, :]
                out = diags[c, z, inner, :] * v[lead, c, z + 1, inner, :]
                for k, e in zip(others, couple):
                    out = out + (0.125 * tens[e, z, inner, :]) * v[lead, k, z + 1, inner, :]
                near = m * neighbour_sum(v, (lead, c), z + 1, start, size) + neighbour_sum(
                    g, (lead, c), z + 1, start, size
                )
                store(z, start, size, m, out - 0.0625 * near)
            return carry

        lax.fori_loop(0, depth, body, 0)

    def apply_whole(stage, r, c):
        def store(z, start, size, m, out):
            inner = pl.ds(PAD + start, size)
            if stage == 0:
                v1[r, c, z + 1, inner, :] = out
                g1[r, c, z + 1, inner, :] = m * out
            else:
                filt[r, c * depth + z, pl.ds(start, size), :] = 2.0 * out - v0[r, c, z + 1, inner, :]

        chunks = [(start, rows) for start in range(0, height, rows)]
        v, g = ((v0, g0), (v1, g1))[stage]
        apply(v, g, (mod, diag, ten), r, c, chunks, store)

    def apply_quarter(stage, source, c):
        def store(z, start, size, m, out):
            inner = pl.ds(PAD + start, size)
            if stage == 0:
                t1[source, c, z + 1, inner, :] = out
            else:
                every[source * mine + first, c * depth + z] = 2.0 * out - t0[source, c, z + 1, inner, :]

        chunks = [(-4, share + 8)] if stage == 0 else [(0, share)]
        v, g = ((t0, h0), (t1, h1))[stage]
        apply(v, g, (tmod, tdiag, tten), source, c, chunks, store)

    def quarter_products(stage, source):
        v, g = ((t0, h0), (t1, h1))[stage]
        for c in range(3):
            for plane in range(depth + 2):
                g[source, c, plane] = tmod[plane] * v[source, c, plane]

    def wait_halo(stage, r, c):
        v, g = ((v0, g0), (v1, g1))[stage]
        for way in range(2):
            guarded(can_recv[way], lambda way=way: halo_copy(stage, r, c, way).wait_recv())
            plane = lands[way]
            g[r, c, plane] = mod[plane] * v[r, c, plane]

    def there_copy(r, c, o):
        to = lax.rem(group + o, groups)
        part = pl.ds(c * depth, depth)
        return pltpu.make_async_remote_copy(
            src_ref=filt.at[r, part, pl.ds(pl.multiple_of(to * share, share), share), :],
            dst_ref=every.at[group * mine + r, part],
            send_sem=there_send.at[r, c, o],
            recv_sem=there_recv.at[r, c, o],
            device_id={"probe": to},
            device_id_type=MESH,
        )

    own_rows = pl.ds(pl.multiple_of(group * share, share), share)

    def keep_copy(r):
        return pltpu.make_async_copy(filt.at[r, :, own_rows, :], every.at[group * mine + r], own_sem.at[r])

    for r in range(first):
        loads[3 + r].wait()
        for c in range(3):
            for z in range(1, depth + 1):
                g0[r, c, z] = mod[z] * v0[r, c, z]
                blank = jnp.zeros((PAD, LANES), jnp.float32)
                g1[r, c, z, pl.ds(0, PAD), :] = blank
                g1[r, c, z, pl.ds(PAD + height, PAD), :] = blank
        for c in range(3):
            wait_halo(0, r, c)
            apply_whole(0, r, c)
            for way in range(2):
                guarded(can_send[way], lambda way=way, r=r, c=c: halo_copy(1, r, c, way).start())
        if r + 1 < first:
            send_probe(r + 1)

    take = pl.ds(pl.multiple_of(group * share, share), wide)
    for plane in range(depth + 2):
        tmod[plane] = mod[plane, take, :]
    for z in range(depth):
        for e in range(6):
            tten[e, z] = ten[e, z, take, :]
        for c in range(3):
            tdiag[c, z] = diag[c, z, take, :]

    for kind in range(3):
        maybe(in_mesh(kind, group), lambda kind=kind: raw_local(kind).wait())
    quarter_send_all(0, 0)
    for o in order:
        for kind in range(3):
            maybe(in_mesh(kind, group), lambda kind=kind, o=o: raw_copy(kind, o, True).wait_recv())
        quarter_send_all(0, o)

    for r in range(first):
        for c in range(3):
            wait_halo(1, r, c)
            apply_whole(1, r, c)
            for o in order:
                there_copy(r, c, o).start()
        keep_copy(r).start()

    def source_of(o):
        return lax.rem(group + groups - o, groups)

    for o in [0] + order:
        quarter_wait(0, o)
        quarter_products(0, source_of(o))
        for c in range(3):
            apply_quarter(0, source_of(o), c)

        def drop(start, o=o):
            t1[source_of(o), :, pl.ds(1, depth), pl.ds(start, PAD), :] = jnp.zeros(
                (3, depth, PAD, LANES), jnp.float32
            )

        guarded(group == 0, lambda drop=drop: drop(0))
        guarded(group == groups - 1, lambda drop=drop: drop(PAD + share))
        quarter_send_all(1, o)

    loads[2].wait()
    for i in range(0, known, GROUP):
        for j in range(i, known, GROUP):
            left = list(range(i, i + GROUP))
            right = list(range(j, j + GROUP))
            products(
                [(quick, k) for k in left], [(quick, k) for k in right], acc_q, right, left,
                (lambda a, b, left=left, right=right: (right[b], left[a])) if i != j else None,
                0, fields, True,
            )
    share_start(slots_q, "slab", slab, slabs, sum_send.at[0], sum_recv.at[0], collapse(acc_q, known, known))

    for o in [0] + order:
        quarter_wait(1, o)
        quarter_products(1, source_of(o))
        for c in range(3):
            apply_quarter(1, source_of(o), c)

    partial = share_finish(slots_q, "slab", slab, slabs, sum_send.at[0], sum_recv.at[0])
    share_start(slots_qp, "probe", group, groups, sump_send.at[0], sump_recv.at[0], partial)

    gram_q = share_finish(slots_qp, "probe", group, groups, sump_send.at[0], sump_recv.at[0])
    square = (known, LANES)
    lane = lax.broadcasted_iota(jnp.int32, square, 1)
    line = lax.broadcasted_iota(jnp.int32, square, 0)
    table = jnp.where(lane < known, gram_q, 0.0) + jnp.where(lane == line + known, 1.0, 0.0)
    for k in range(known):
        column = spread(table[:, k : k + 1], square)
        pivot = spread(column[k : k + 1, :], square)
        lead = spread(table[k : k + 1, :], square) / pivot
        table = jnp.where(line == k, lead, table - column * lead)
    inverse[...] = pltpu.roll(table, LANES - known, 1)
    inv = jnp.where(lane < known, inverse[...], 0.0)
    inverse[...] = inv

    def batch(r):
        ids = [p * mine + r for p in range(groups)]
        return [ids[i : i + GROUP] for i in range(0, groups, GROUP)]

    sequence = [first] + list(range(first))
    for turn, r in enumerate(sequence):
        if r < first:
            keep_copy(r).wait()
        for c in range(3):
            if r < first:
                for o in order:
                    there_copy(r, c, o).wait_recv()
            span = (c * depth, (c + 1) * depth, c == 0)
            for ids in batch(r):
                for i in range(0, known, GROUP):
                    left = list(range(i, i + GROUP))
                    products([(quick, k) for k in left], [(every, k) for k in ids], acc_y, ids, left, None, *span)
                for before in sequence[: turn + 1]:
                    for old in batch(before):
                        if before == r and old[0] > ids[0]:
                            continue
                        same = old == ids
                        products(
                            [(every, k) for k in old], [(every, k) for k in ids], acc_y, ids,
                            [known + k for k in old],
                            None if same else (lambda a, b, old=old, ids=ids: (known + ids[b], old[a])),
                            *span,
                        )
    part = collapse(acc_y, known + total, total)
    share_start(slots_y, "slab", slab, slabs, sum_send.at[1], sum_recv.at[1], part)
    part = share_finish(slots_y, "slab", slab, slabs, sum_send.at[1], sum_recv.at[1])
    share_start(slots_yp, "probe", group, groups, sump_send.at[1], sump_recv.at[1], part)
    gram_y = share_finish(slots_yp, "probe", group, groups, sump_send.at[1], sump_recv.at[1])

    flat = (total, LANES)
    lane = lax.broadcasted_iota(jnp.int32, flat, 1)
    line = lax.broadcasted_iota(jnp.int32, flat, 0)
    cross = jnp.where(lane < known, gram_y, 0.0)
    coeff = jnp.zeros(flat, jnp.float32)
    for k in range(known):
        coeff = coeff + spread(cross[:, k : k + 1], flat) * spread(inverse[k : k + 1, :], flat)
    nt = (((1,), (1,)), ((), ()))
    taken = lax.dot_general(
        coeff, jnp.concatenate([cross, jnp.zeros((LANES - total, LANES), jnp.float32)], axis=0), nt,
        precision=lax.Precision.HIGHEST, preferred_element_type=jnp.float32,
    )
    at = known + total
    gram = pltpu.roll(gram_y, LANES - known, 1) - taken
    gram = jnp.where(lane < total, gram, 0.0)
    work = pltpu.roll(gram, at, 1) + jnp.where(lane == line + known, 1.0, 0.0) - coeff
    factor = jnp.ones(flat, jnp.float32)
    for k in range(total):
        column = spread(work[:, at + k : at + k + 1], flat)
        pivot = spread(column[k : k + 1, :], flat)
        lead = spread(work[k : k + 1, :], flat) / pivot
        factor = jnp.where(line == k, pivot, factor)
        work = jnp.where(line > k, work - column * lead, work)
    mixing[...] = work / jnp.sqrt(factor)

    def make(i):
        weights = mixing[pl.ds(i, 1), :]
        splats = [spread(weights[:, v : v + 1], (8, LANES)) for v in range(known + total)]

        def step(f, carry):
            for t in range(share // 8):
                sub = pl.ds(8 * t, 8)
                value = splats[0] * quick[0, f, sub, :]
                for v in range(1, known):
                    value = value + splats[v] * quick[v, f, sub, :]
                for v in range(total):
                    value = value + splats[known + v] * every[v, f, sub, :]
                outgoing[i, f, sub, :] = value
            return carry

        lax.fori_loop(0, fields, step, 0)

    def back_copy(r, o):
        to = lax.rem(group + o, groups)
        return pltpu.make_async_remote_copy(
            src_ref=outgoing.at[to * mine + r],
            dst_ref=basis_ref.at[r, :, own_rows, :],
            send_sem=back_send.at[r, o],
            recv_sem=back_recv.at[r, o],
            device_id={"probe": to},
            device_id_type=MESH,
        )

    def own_copy(r):
        return pltpu.make_async_copy(
            outgoing.at[group * mine + r], basis_ref.at[r, :, own_rows, :], own_sem.at[mine + r]
        )

    for o in order:
        for r in range(mine):
            make(lax.rem(group + o, groups) * mine + r)
            back_copy(r, o).start()
    for r in range(mine):
        make(group * mine + r)
        own_copy(r).start()

    corr_ref[...] = coeff[:, :known]

    for way in range(2):
        def finish(way=way):
            mod_copy(way).wait_send()
            for stage in range(2):
                for r in range(first):
                    for c in range(3):
                        halo_copy(stage, r, c, way).wait_send()
                for o in range(groups):
                    quarter_copy(stage, o, way).wait_send()
        guarded(can_send[way], finish)
    for r in range(mine):
        own_copy(r).wait()
        for o in order:
            if r < first:
                for c in range(3):
                    there_copy(r, c, o).wait_send()
            back_copy(r, o).wait()
    for o in order:
        to = lax.rem(group + o, groups)
        for kind in range(3):
            maybe(in_mesh(kind, to), lambda kind=kind, o=o: raw_copy(kind, o).wait_send())


def body(probes, earlier, modulus, tangent):
    mine, parts, depth, height, width = probes.shape
    known, _, _, share, _ = earlier.shape
    slabs = lax.axis_size("slab")
    groups = lax.axis_size("probe")
    total = mine * groups
    fields = parts * depth
    scale = float(parts * depth * slabs * height * width) ** 0.5
    f32 = jnp.float32
    padded = (mine - 1, parts, depth + 2, height + 2 * PAD, width)
    quarter = (groups, parts, depth + 2, share + 2 * PAD, width)
    dma = pltpu.SemaphoreType.DMA
    anywhere = pl.BlockSpec(memory_space=pltpu.HBM)
    basis, corr = pl.pallas_call(
        functools.partial(kernel, slabs, groups),
        out_shape=(
            jax.ShapeDtypeStruct((mine, fields, height, width), f32),
            jax.ShapeDtypeStruct((total, known), f32),
        ),
        in_specs=[anywhere] * 4,
        out_specs=(anywhere, pl.BlockSpec(memory_space=pltpu.VMEM)),
        scratch_shapes=[
            pltpu.VMEM(padded, f32),
            pltpu.VMEM(padded, f32),
            pltpu.VMEM(padded, f32),
            pltpu.VMEM(padded, f32),
            pltpu.VMEM(quarter, f32),
            pltpu.VMEM(quarter, f32),
            pltpu.VMEM(quarter, f32),
            pltpu.VMEM(quarter, f32),
            pltpu.VMEM((depth + 2, height + 2 * PAD, width), f32),
            pltpu.VMEM((6, depth, height + 2 * PAD, width), f32),
            pltpu.VMEM((3, depth, height + 2 * PAD, width), f32),
            pltpu.VMEM((depth + 2, share + 2 * PAD, width), f32),
            pltpu.VMEM((6, depth, share + 2 * PAD, width), f32),
            pltpu.VMEM((3, depth, share + 2 * PAD, width), f32),
            pltpu.VMEM((known, fields, share, width), f32),
            pltpu.VMEM((mine, fields, height, width), f32),
            pltpu.VMEM((total, fields, share, width), f32),
            pltpu.VMEM((total, fields, share, width), f32),
            pltpu.VMEM((known, known, 8, width), f32),
            pltpu.VMEM((known + total, total, 8, width), f32),
            pltpu.VMEM((slabs, known, LANES), f32),
            pltpu.VMEM((groups, known, LANES), f32),
            pltpu.VMEM((slabs, total, LANES), f32),
            pltpu.VMEM((groups, total, LANES), f32),
            pltpu.VMEM((known, LANES), f32),
            pltpu.VMEM((total, LANES), f32),
            dma((3 + mine,)),
            dma((2, mine, parts, 2)),
            dma((2, mine, parts, 2)),
            dma((2,)),
            dma((2,)),
            dma((mine, parts, groups)),
            dma((mine, parts, groups)),
            dma((mine, groups)),
            dma((mine, groups)),
            dma((2, slabs)),
            dma((2, slabs)),
            dma((2, groups)),
            dma((2, groups)),
            dma((2 * mine,)),
            dma((3, groups)),
            dma((3, groups)),
            dma((3,)),
            dma((2, groups, 2)),
            dma((2, groups, 2)),
        ],
        compiler_params=pltpu.CompilerParams(
            collective_id=0, has_side_effects=True, vmem_limit_bytes=60 * 1024 * 1024
        ),
    )(probes, earlier.reshape(known, fields, share, width), modulus, tangent)
    return basis.reshape(probes.shape) * scale, corr.T * scale


def solution(mesh):
    in_specs = (
        P("probe", None, "slab", None, None),
        P(None, None, "slab", "probe", None),
        P("slab", None, None),
        P(None, "slab", None, None),
    )
    out_specs = (P("probe", None, "slab", None, None), P())
    return jax.shard_map(body, mesh=mesh, in_specs=in_specs, out_specs=out_specs, check_vma=False)
```

```python
import functools

import jax
import jax.numpy as jnp
from jax import lax
from jax.experimental import pallas as pl
from jax.experimental.pallas import tpu as pltpu
from jax.sharding import PartitionSpec as P

MESH = pl.DeviceIdType.MESH
LANES = 128
PAD = 8
GROUP = 4
EDGE = 2


def neighbour_sum(ref, lead, z, start, rows):
    def at(plane, off):
        return ref[lead + (plane, pl.ds(PAD + start + off, rows), slice(None))]

    centre = at(z, 0)
    beside = at(z, -1) + at(z, 1)
    above = at(z - 1, 0) + at(z + 1, 0)
    corner = (at(z - 1, -1) + at(z + 1, -1)) + (at(z - 1, 1) + at(z + 1, 1))
    along = 0.3 * centre + 0.1 * (above + beside) + 0.05 * corner
    still = 0.3 * (above + beside) + 0.1 * corner
    width = along.shape[-1]
    lane = lax.broadcasted_iota(jnp.int32, along.shape, 1)
    from_left = jnp.where(lane == 0, 0.0, pltpu.roll(along, 1, 1))
    from_right = jnp.where(lane == width - 1, 0.0, pltpu.roll(along, width - 1, 1))
    return still + from_left + from_right


def spread(column, shape):
    return jnp.broadcast_to(column, shape)


def kernel(
    slabs, groups,
    probes_ref, earlier_ref, modulus_ref, tangent_ref,
    basis_ref, corr_ref,
    v0, v1, g0, g1, t0, t1, h0, h1, mod, ten, diag, tmod, tten, tdiag, quick, filt, every, outgoing,
    acc_q, acc_y, slots_q, slots_qp, slots_y, slots_yp, inverse, mixing,
    load_sem, halo_send, halo_recv, mod_send, mod_recv,
    there_send, there_recv, back_send, back_recv,
    sum_send, sum_recv, sump_send, sump_recv, own_sem,
    raw_send, raw_recv, raw_own, quarter_send, quarter_recv,
):
    slab = lax.axis_index("slab")
    group = lax.axis_index("probe")
    mine, _, depth, height, _ = probes_ref.shape
    known, fields, share, _ = earlier_ref.shape
    total = mine * groups
    rows = 32
    first = mine - 1
    wide = share + 2 * PAD

    loads = [
        pltpu.make_async_copy(modulus_ref, mod.at[pl.ds(1, depth), pl.ds(PAD, height), :], load_sem.at[0]),
        pltpu.make_async_copy(tangent_ref, ten.at[:, :, pl.ds(PAD, height), :], load_sem.at[1]),
        pltpu.make_async_copy(earlier_ref, quick, load_sem.at[2]),
    ]
    for r in range(first):
        loads.append(
            pltpu.make_async_copy(
                probes_ref.at[r],
                v0.at[r, :, pl.ds(1, depth), pl.ds(PAD, height), :],
                load_sem.at[3 + r],
            )
        )
    for i in [0] + list(range(3, 3 + first)) + [1, 2]:
        loads[i].start()

    barrier = pltpu.get_barrier_semaphore()
    for o in range(1, slabs):
        pl.semaphore_signal(barrier, inc=1, device_id={"slab": lax.rem(slab + o, slabs)}, device_id_type=MESH)
    for o in range(1, groups):
        pl.semaphore_signal(barrier, inc=1, device_id={"probe": lax.rem(group + o, groups)}, device_id_type=MESH)

    for ref in (v0, v1):
        edge = jnp.zeros(ref.shape[:3] + (PAD, LANES), jnp.float32)
        ref[:, :, :, pl.ds(0, PAD), :] = edge
        ref[:, :, :, pl.ds(PAD + height, PAD), :] = edge
    for ref in (ten, diag):
        edge = jnp.zeros(ref.shape[:2] + (PAD, LANES), jnp.float32)
        ref[:, :, pl.ds(0, PAD), :] = edge
        ref[:, :, pl.ds(PAD + height, PAD), :] = edge
    for ref in (t0, t1):
        edge = jnp.zeros(ref.shape[:3] + (PAD - EDGE, LANES), jnp.float32)
        ref[:, :, :, pl.ds(0, PAD - EDGE), :] = edge
        ref[:, :, :, pl.ds(PAD + share + EDGE, PAD - EDGE), :] = edge
    edge = jnp.zeros((depth + 2, PAD, LANES), jnp.float32)
    mod[:, pl.ds(0, PAD), :] = edge
    mod[:, pl.ds(PAD + height, PAD), :] = edge

    def clear(plane):
        for ref in (v0, v1):
            ref[:, :, plane, pl.ds(PAD, height), :] = jnp.zeros((first, 3, height, LANES), jnp.float32)
        for ref in (t0, t1):
            ref[:, :, plane] = jnp.zeros((groups, 3, wide, LANES), jnp.float32)
        mod[plane, pl.ds(PAD, height), :] = jnp.zeros((height, LANES), jnp.float32)

    def clear_rows(ref, start):
        count = ref.shape[0]
        blank = jnp.zeros((count, 3, depth, EDGE, LANES), jnp.float32)
        ref[:, :, pl.ds(1, depth), pl.ds(start, EDGE), :] = blank

    @pl.when(group == 0)
    def _():
        clear_rows(t0, PAD - EDGE)

    @pl.when(group == groups - 1)
    def _():
        clear_rows(t0, PAD + share)

    @pl.when(slab == 0)
    def _():
        clear(0)

    @pl.when(slab == slabs - 1)
    def _():
        clear(depth + 1)

    pl.semaphore_wait(barrier, slabs + groups - 2)

    towards = (lax.rem(slab + slabs - 1, slabs), lax.rem(slab + 1, slabs))
    can_send = (slab > 0, slab < slabs - 1)
    can_recv = (slab < slabs - 1, slab > 0)
    lands = (depth + 1, 0)

    def mod_copy(way):
        return pltpu.make_async_remote_copy(
            src_ref=modulus_ref.at[(0, depth - 1)[way]],
            dst_ref=mod.at[lands[way], pl.ds(PAD, height), :],
            send_sem=mod_send.at[way],
            recv_sem=mod_recv.at[way],
            device_id={"slab": towards[way]},
            device_id_type=MESH,
        )

    def halo_copy(stage, r, c, way):
        if stage == 0:
            source, into = probes_ref.at[r, c, (0, depth - 1)[way]], v0
        else:
            source, into = v1.at[r, c, (1, depth)[way], pl.ds(PAD, height), :], v1
        return pltpu.make_async_remote_copy(
            src_ref=source,
            dst_ref=into.at[r, c, lands[way], pl.ds(PAD, height), :],
            send_sem=halo_send.at[stage, r, c, way],
            recv_sem=halo_recv.at[stage, r, c, way],
            device_id={"slab": towards[way]},
            device_id_type=MESH,
        )

    def guarded(condition, act):
        @pl.when(condition)
        def _():
            act()

    def send_probe(r):
        for way in range(2):
            def begin(way=way):
                if r == 0:
                    mod_copy(way).start()
                for c in range(3):
                    halo_copy(0, r, c, way).start()
            guarded(can_send[way], begin)

    def raw_part(kind, to):
        return (
            pl.ds(pl.multiple_of(to * share, share), share),
            pl.ds(to * share - EDGE, EDGE),
            pl.ds(to * share + share, EDGE),
        )[kind]

    raw_rows = (pl.ds(PAD, share), pl.ds(PAD - EDGE, EDGE), pl.ds(PAD + share, EDGE))

    def raw_copy(kind, o, arriving=False):
        to = lax.rem(group + o, groups)
        landing = t0.at[group, :, pl.ds(1, depth), raw_rows[kind], :]
        return pltpu.make_async_remote_copy(
            src_ref=landing if arriving else probes_ref.at[first, :, :, raw_part(kind, to), :],
            dst_ref=t0.at[group, :, pl.ds(1, depth), raw_rows[kind], :],
            send_sem=raw_send.at[kind, o],
            recv_sem=raw_recv.at[kind, o],
            device_id={"probe": to},
            device_id_type=MESH,
        )

    def raw_local(kind):
        return pltpu.make_async_copy(
            probes_ref.at[first, :, :, raw_part(kind, group), :],
            t0.at[group, :, pl.ds(1, depth), raw_rows[kind], :],
            raw_own.at[kind],
        )

    def in_mesh(kind, to):
        return (None, to > 0, to < groups - 1)[kind]

    def maybe(condition, act):
        if condition is None:
            act()
        else:
            guarded(condition, act)

    order = sorted(range(1, groups), key=lambda o: (abs(o - groups // 2), o))

    send_probe(0)
    for kind in range(3):
        maybe(in_mesh(kind, group), lambda kind=kind: raw_local(kind).start())
    for o in order:
        to = lax.rem(group + o, groups)
        for kind in range(3):
            maybe(in_mesh(kind, to), lambda kind=kind, o=o: raw_copy(kind, o).start())

    def quarter_copy(stage, o, way):
        ref = (t0, t1)[stage]
        source = lax.rem(group + groups - o, groups)
        span = pl.ds(PAD - EDGE, share + 2 * EDGE)
        return pltpu.make_async_remote_copy(
            src_ref=ref.at[source, :, (1, depth)[way], span, :],
            dst_ref=ref.at[source, :, lands[way], span, :],
            send_sem=quarter_send.at[stage, o, way],
            recv_sem=quarter_recv.at[stage, o, way],
            device_id={"slab": towards[way]},
            device_id_type=MESH,
        )

    def quarter_send_all(stage, o):
        for way in range(2):
            guarded(can_send[way], lambda way=way: quarter_copy(stage, o, way).start())

    def quarter_wait(stage, o):
        for way in range(2):
            guarded(can_recv[way], lambda way=way: quarter_copy(stage, o, way).wait_recv())

    def products(first, second, acc_ref, rows_at, cols_at, mirror_at, begin, end, fresh):
        def step(f, accs):
            left = [ref[k, f] for ref, k in first]
            right = [ref[k, f] for ref, k in second]
            out = []
            n = 0
            for a in left:
                for b in right:
                    prod = a * b
                    part = accs[n]
                    for t in range(share // 8):
                        part = part + prod[8 * t : 8 * t + 8]
                    out.append(part)
                    n += 1
            return tuple(out)

        zero = jnp.zeros((8, LANES), jnp.float32)
        if fresh:
            accs = (zero,) * (len(first) * len(second))
        else:
            accs = tuple(acc_ref[col, row] for col in cols_at for row in rows_at)
        accs = lax.fori_loop(begin, end, step, accs)
        n = 0
        for i in range(len(first)):
            for j in range(len(second)):
                acc_ref[cols_at[i], rows_at[j]] = accs[n]
                if mirror_at is not None:
                    col, row = mirror_at(i, j)
                    acc_ref[col, row] = accs[n]
                n += 1

    def collapse(acc_ref, cols, count):
        lane = lax.broadcasted_iota(jnp.int32, (count, LANES), 1)
        result = jnp.zeros((count, LANES), jnp.float32)
        for v in range(cols):
            summed = jnp.sum(jnp.sum(acc_ref[v], axis=1), axis=1, keepdims=True)
            result = jnp.where(lane == v, spread(summed, (count, LANES)), result)
        return result

    def share_copy(slots, axis, me, count, o, sends, recvs):
        return pltpu.make_async_remote_copy(
            src_ref=slots.at[me],
            dst_ref=slots.at[me],
            send_sem=sends.at[o],
            recv_sem=recvs.at[o],
            device_id={axis: lax.rem(me + o, count)},
            device_id_type=MESH,
        )

    def share_start(slots, axis, me, count, sends, recvs, value):
        slots[me] = value
        for o in range(1, count):
            share_copy(slots, axis, me, count, o, sends, recvs).start()

    def share_finish(slots, axis, me, count, sends, recvs):
        for o in range(1, count):
            share_copy(slots, axis, me, count, o, sends, recvs).wait()
        value = slots[0]
        for i in range(1, count):
            value = value + slots[i]
        return value

    loads[0].wait()
    loads[1].wait()
    for way in range(2):
        guarded(can_recv[way], lambda way=way: mod_copy(way).wait_recv())

    def coefficients(z, carry):
        for start in range(0, height, rows):
            here = pl.ds(PAD + start, rows)
            m = mod[z + 1, here, :]
            base = (3.4 * m + neighbour_sum(mod, (), z + 1, start, rows)) * 0.0625 - 1.0
            for c in range(3):
                diag[c, z, here, :] = base + 0.125 * ten[c, z, here, :]
        return carry

    lax.fori_loop(0, depth, coefficients, 0)

    def apply(v, g, fields_of, lead, c, chunks, store):
        mods, diags, tens = fields_of
        others = [k for k in range(3) if k != c]
        couple = [3 + c + k - 1 for k in others]

        def body(z, carry):
            for start, size in chunks:
                inner = pl.ds(PAD + start, size)
                m = mods[z + 1, inner, :]
                out = diags[c, z, inner, :] * v[lead, c, z + 1, inner, :]
                for k, e in zip(others, couple):
                    out = out + (0.125 * tens[e, z, inner, :]) * v[lead, k, z + 1, inner, :]
                near = m * neighbour_sum(v, (lead, c), z + 1, start, size) + neighbour_sum(
                    g, (lead, c), z + 1, start, size
                )
                store(z, start, size, m, out - 0.0625 * near)
            return carry

        lax.fori_loop(0, depth, body, 0)

    def apply_whole(stage, r, c):
        def store(z, start, size, m, out):
            inner = pl.ds(PAD + start, size)
            if stage == 0:
                v1[r, c, z + 1, inner, :] = out
                g1[r, c, z + 1, inner, :] = m * out
            else:
                filt[r, c * depth + z, pl.ds(start, size), :] = 2.0 * out - v0[r, c, z + 1, inner, :]

        chunks = [(start, rows) for start in range(0, height, rows)]
        v, g = ((v0, g0), (v1, g1))[stage]
        apply(v, g, (mod, diag, ten), r, c, chunks, store)

    def apply_quarter(stage, source, c):
        def store(z, start, size, m, out):
            inner = pl.ds(PAD + start, size)
            if stage == 0:
                t1[source, c, z + 1, inner, :] = out
            else:
                every[source * mine + first, c * depth + z] = 2.0 * out - t0[source, c, z + 1, inner, :]

        chunks = [(-4, share + 8)] if stage == 0 else [(0, share)]
        v, g = ((t0, h0), (t1, h1))[stage]
        apply(v, g, (tmod, tdiag, tten), source, c, chunks, store)

    def quarter_products(stage, source):
        v, g = ((t0, h0), (t1, h1))[stage]
        for c in range(3):
            for plane in range(depth + 2):
                g[source, c, plane] = tmod[plane] * v[source, c, plane]

    def wait_halo(stage, r, c):
        v, g = ((v0, g0), (v1, g1))[stage]
        for way in range(2):
            guarded(can_recv[way], lambda way=way: halo_copy(stage, r, c, way).wait_recv())
            plane = lands[way]
            g[r, c, plane] = mod[plane] * v[r, c, plane]

    def there_copy(r, c, o):
        to = lax.rem(group + o, groups)
        part = pl.ds(c * depth, depth)
        return pltpu.make_async_remote_copy(
            src_ref=filt.at[r, part, pl.ds(pl.multiple_of(to * share, share), share), :],
            dst_ref=every.at[group * mine + r, part],
            send_sem=there_send.at[r, c, o],
            recv_sem=there_recv.at[r, c, o],
            device_id={"probe": to},
            device_id_type=MESH,
        )

    own_rows = pl.ds(pl.multiple_of(group * share, share), share)

    def keep_copy(r):
        return pltpu.make_async_copy(filt.at[r, :, own_rows, :], every.at[group * mine + r], own_sem.at[r])

    for r in range(first):
        loads[3 + r].wait()
        for c in range(3):
            for z in range(1, depth + 1):
                g0[r, c, z] = mod[z] * v0[r, c, z]
                blank = jnp.zeros((PAD, LANES), jnp.float32)
                g1[r, c, z, pl.ds(0, PAD), :] = blank
                g1[r, c, z, pl.ds(PAD + height, PAD), :] = blank
        for c in range(3):
            wait_halo(0, r, c)
            apply_whole(0, r, c)
            for way in range(2):
                guarded(can_send[way], lambda way=way, r=r, c=c: halo_copy(1, r, c, way).start())
        if r + 1 < first:
            send_probe(r + 1)

    for kind in range(3):
        maybe(in_mesh(kind, group), lambda kind=kind: raw_local(kind).wait())
    quarter_send_all(0, 0)

    loads[2].wait()
    for i in range(0, known, GROUP):
        for j in range(i, known, GROUP):
            left = list(range(i, i + GROUP))
            right = list(range(j, j + GROUP))
            products(
                [(quick, k) for k in left], [(quick, k) for k in right], acc_q, right, left,
                (lambda a, b, left=left, right=right: (right[b], left[a])) if i != j else None,
                0, fields, True,
            )
    share_start(slots_q, "slab", slab, slabs, sum_send.at[0], sum_recv.at[0], collapse(acc_q, known, known))

    for r in range(first):
        for c in range(3):
            wait_halo(1, r, c)
            apply_whole(1, r, c)
            for o in order:
                there_copy(r, c, o).start()
        keep_copy(r).start()

    for o in order:
        for kind in range(3):
            maybe(in_mesh(kind, group), lambda kind=kind, o=o: raw_copy(kind, o, True).wait_recv())
        quarter_send_all(0, o)


    partial = share_finish(slots_q, "slab", slab, slabs, sum_send.at[0], sum_recv.at[0])
    share_start(slots_qp, "probe", group, groups, sump_send.at[0], sump_recv.at[0], partial)

    take = pl.ds(pl.multiple_of(group * share, share), wide)
    for plane in range(depth + 2):
        tmod[plane] = mod[plane, take, :]
    for z in range(depth):
        for e in range(6):
            tten[e, z] = ten[e, z, take, :]
        for c in range(3):
            tdiag[c, z] = diag[c, z, take, :]

    def source_of(o):
        return lax.rem(group + groups - o, groups)

    for o in [0] + order:
        quarter_wait(0, o)
        quarter_products(0, source_of(o))
        for c in range(3):
            apply_quarter(0, source_of(o), c)

        def drop(start, o=o):
            t1[source_of(o), :, pl.ds(1, depth), pl.ds(start, PAD), :] = jnp.zeros(
                (3, depth, PAD, LANES), jnp.float32
            )

        guarded(group == 0, lambda drop=drop: drop(0))
        guarded(group == groups - 1, lambda drop=drop: drop(PAD + share))
        quarter_send_all(1, o)

    gram_q = share_finish(slots_qp, "probe", group, groups, sump_send.at[0], sump_recv.at[0])
    square = (known, LANES)
    lane = lax.broadcasted_iota(jnp.int32, square, 1)
    line = lax.broadcasted_iota(jnp.int32, square, 0)
    table = jnp.where(lane < known, gram_q, 0.0) + jnp.where(lane == line + known, 1.0, 0.0)
    for k in range(known):
        column = spread(table[:, k : k + 1], square)
        pivot = spread(column[k : k + 1, :], square)
        lead = spread(table[k : k + 1, :], square) / pivot
        table = jnp.where(line == k, lead, table - column * lead)
    inverse[...] = pltpu.roll(table, LANES - known, 1)
    inv = jnp.where(lane < known, inverse[...], 0.0)
    inverse[...] = inv

    def last_stage(o):
        quarter_wait(1, o)
        quarter_products(1, source_of(o))
        for c in range(3):
            apply_quarter(1, source_of(o), c)

    def batch(r):
        ids = [p * mine + r for p in range(groups)]
        return [ids[i : i + GROUP] for i in range(0, groups, GROUP)]

    def gather(r):
        if r < first:
            keep_copy(r).wait()
        for c in range(3):
            if r < first:
                for o in order:
                    there_copy(r, c, o).wait_recv()
            span = (c * depth, (c + 1) * depth, c == 0)
            for ids in batch(r):
                for i in range(0, known, GROUP):
                    left = list(range(i, i + GROUP))
                    products([(quick, k) for k in left], [(every, k) for k in ids], acc_y, ids, left, None, *span)
                for before in range(r + 1):
                    for old in batch(before):
                        if before == r and old[0] > ids[0]:
                            continue
                        same = old == ids
                        products(
                            [(every, k) for k in old], [(every, k) for k in ids], acc_y, ids,
                            [known + k for k in old],
                            None if same else (lambda a, b, old=old, ids=ids: (known + ids[b], old[a])),
                            *span,
                        )
    for o in ([0] + order)[:-1]:
        last_stage(o)
    for r in range(first):
        gather(r)
    last_stage(order[-1])
    gather(first)
    part = collapse(acc_y, known + total, total)
    share_start(slots_y, "slab", slab, slabs, sum_send.at[1], sum_recv.at[1], part)
    part = share_finish(slots_y, "slab", slab, slabs, sum_send.at[1], sum_recv.at[1])
    share_start(slots_yp, "probe", group, groups, sump_send.at[1], sump_recv.at[1], part)
    gram_y = share_finish(slots_yp, "probe", group, groups, sump_send.at[1], sump_recv.at[1])

    flat = (total, LANES)
    lane = lax.broadcasted_iota(jnp.int32, flat, 1)
    line = lax.broadcasted_iota(jnp.int32, flat, 0)
    cross = jnp.where(lane < known, gram_y, 0.0)
    coeff = jnp.zeros(flat, jnp.float32)
    for k in range(known):
        coeff = coeff + spread(cross[:, k : k + 1], flat) * spread(inverse[k : k + 1, :], flat)
    nt = (((1,), (1,)), ((), ()))
    taken = lax.dot_general(
        coeff, jnp.concatenate([cross, jnp.zeros((LANES - total, LANES), jnp.float32)], axis=0), nt,
        precision=lax.Precision.HIGHEST, preferred_element_type=jnp.float32,
    )
    at = known + total
    gram = pltpu.roll(gram_y, LANES - known, 1) - taken
    gram = jnp.where(lane < total, gram, 0.0)
    work = pltpu.roll(gram, at, 1) + jnp.where(lane == line + known, 1.0, 0.0) - coeff
    factor = jnp.ones(flat, jnp.float32)
    for k in range(total):
        column = spread(work[:, at + k : at + k + 1], flat)
        pivot = spread(column[k : k + 1, :], flat)
        lead = spread(work[k : k + 1, :], flat) / pivot
        factor = jnp.where(line == k, pivot, factor)
        work = jnp.where(line > k, work - column * lead, work)
    mixing[...] = work / jnp.sqrt(factor)

    def make(i):
        weights = mixing[pl.ds(i, 1), :]
        splats = [spread(weights[:, v : v + 1], (8, LANES)) for v in range(known + total)]

        def step(f, carry):
            for t in range(share // 8):
                sub = pl.ds(8 * t, 8)
                value = splats[0] * quick[0, f, sub, :]
                for v in range(1, known):
                    value = value + splats[v] * quick[v, f, sub, :]
                for v in range(total):
                    value = value + splats[known + v] * every[v, f, sub, :]
                outgoing[i, f, sub, :] = value
            return carry

        lax.fori_loop(0, fields, step, 0)

    def back_copy(r, o):
        to = lax.rem(group + o, groups)
        return pltpu.make_async_remote_copy(
            src_ref=outgoing.at[to * mine + r],
            dst_ref=basis_ref.at[r, :, own_rows, :],
            send_sem=back_send.at[r, o],
            recv_sem=back_recv.at[r, o],
            device_id={"probe": to},
            device_id_type=MESH,
        )

    def own_copy(r):
        return pltpu.make_async_copy(
            outgoing.at[group * mine + r], basis_ref.at[r, :, own_rows, :], own_sem.at[mine + r]
        )

    for o in order:
        for r in range(mine):
            make(lax.rem(group + o, groups) * mine + r)
            back_copy(r, o).start()
    for r in range(mine):
        make(group * mine + r)
        own_copy(r).start()

    corr_ref[...] = coeff[:, :known]

    for way in range(2):
        def finish(way=way):
            mod_copy(way).wait_send()
            for stage in range(2):
                for r in range(first):
                    for c in range(3):
                        halo_copy(stage, r, c, way).wait_send()
                for o in range(groups):
                    quarter_copy(stage, o, way).wait_send()
        guarded(can_send[way], finish)
    for r in range(mine):
        own_copy(r).wait()
        for o in order:
            if r < first:
                for c in range(3):
                    there_copy(r, c, o).wait_send()
            back_copy(r, o).wait()
    for o in order:
        to = lax.rem(group + o, groups)
        for kind in range(3):
            maybe(in_mesh(kind, to), lambda kind=kind, o=o: raw_copy(kind, o).wait_send())


def body(probes, earlier, modulus, tangent):
    mine, parts, depth, height, width = probes.shape
    known, _, _, share, _ = earlier.shape
    slabs = lax.axis_size("slab")
    groups = lax.axis_size("probe")
    total = mine * groups
    fields = parts * depth
    scale = float(parts * depth * slabs * height * width) ** 0.5
    f32 = jnp.float32
    padded = (mine - 1, parts, depth + 2, height + 2 * PAD, width)
    quarter = (groups, parts, depth + 2, share + 2 * PAD, width)
    dma = pltpu.SemaphoreType.DMA
    anywhere = pl.BlockSpec(memory_space=pltpu.HBM)
    basis, corr = pl.pallas_call(
        functools.partial(kernel, slabs, groups),
        out_shape=(
            jax.ShapeDtypeStruct((mine, fields, height, width), f32),
            jax.ShapeDtypeStruct((total, known), f32),
        ),
        in_specs=[anywhere] * 4,
        out_specs=(anywhere, pl.BlockSpec(memory_space=pltpu.VMEM)),
        scratch_shapes=[
            pltpu.VMEM(padded, f32),
            pltpu.VMEM(padded, f32),
            pltpu.VMEM(padded, f32),
            pltpu.VMEM(padded, f32),
            pltpu.VMEM(quarter, f32),
            pltpu.VMEM(quarter, f32),
            pltpu.VMEM(quarter, f32),
            pltpu.VMEM(quarter, f32),
            pltpu.VMEM((depth + 2, height + 2 * PAD, width), f32),
            pltpu.VMEM((6, depth, height + 2 * PAD, width), f32),
            pltpu.VMEM((3, depth, height + 2 * PAD, width), f32),
            pltpu.VMEM((depth + 2, share + 2 * PAD, width), f32),
            pltpu.VMEM((6, depth, share + 2 * PAD, width), f32),
            pltpu.VMEM((3, depth, share + 2 * PAD, width), f32),
            pltpu.VMEM((known, fields, share, width), f32),
            pltpu.VMEM((mine, fields, height, width), f32),
            pltpu.VMEM((total, fields, share, width), f32),
            pltpu.VMEM((total, fields, share, width), f32),
            pltpu.VMEM((known, known, 8, width), f32),
            pltpu.VMEM((known + total, total, 8, width), f32),
            pltpu.VMEM((slabs, known, LANES), f32),
            pltpu.VMEM((groups, known, LANES), f32),
            pltpu.VMEM((slabs, total, LANES), f32),
            pltpu.VMEM((groups, total, LANES), f32),
            pltpu.VMEM((known, LANES), f32),
            pltpu.VMEM((total, LANES), f32),
            dma((3 + mine,)),
            dma((2, mine, parts, 2)),
            dma((2, mine, parts, 2)),
            dma((2,)),
            dma((2,)),
            dma((mine, parts, groups)),
            dma((mine, parts, groups)),
            dma((mine, groups)),
            dma((mine, groups)),
            dma((2, slabs)),
            dma((2, slabs)),
            dma((2, groups)),
            dma((2, groups)),
            dma((2 * mine,)),
            dma((3, groups)),
            dma((3, groups)),
            dma((3,)),
            dma((2, groups, 2)),
            dma((2, groups, 2)),
        ],
        compiler_params=pltpu.CompilerParams(
            collective_id=0, has_side_effects=True, vmem_limit_bytes=60 * 1024 * 1024
        ),
    )(probes, earlier.reshape(known, fields, share, width), modulus, tangent)
    return basis.reshape(probes.shape) * scale, corr.T * scale


def solution(mesh):
    in_specs = (
        P("probe", None, "slab", None, None),
        P(None, None, "slab", "probe", None),
        P("slab", None, None),
        P(None, "slab", None, None),
    )
    out_specs = (P("probe", None, "slab", None, None), P())
    return jax.shard_map(body, mesh=mesh, in_specs=in_specs, out_specs=out_specs, check_vma=False)
```
